512 devices in a mesh: seq: 32 (over x, y_hi, core), dp: 16 (over z, y_lo).
Axes of the slice: x: 4, y: 8 (y_hi: 4, y_lo: 2; y = y_hi * 2 + y_lo), z: 8, core: 2. Of those that a mesh axis runs over, the one named last changes fastest.
Arguments:
- queries: bfloat16 [16, 4096, 2048], P('dp', 'seq'), may hold values from -6 to 6
- key_branch: bfloat16 [16, 4096, 2048], P('dp', 'seq'), may hold values from -6 to 6
- value_branch: bfloat16 [16, 4096, 2048], P('dp', 'seq'), may hold values from -6 to 6
- cotangent: bfloat16 [16, 4096, 2048], P('dp', 'seq'), may hold values from -6 to 6
- residues: float32 [16, 2048], replicated, may hold values from -0.046875 to 0.046875
- rates: float32 [16, 2048], replicated, may hold values from 0.2 to 300
- skip_gain: float32 [2048], replicated, may hold values from 0.5 to 1.5
Outputs:
- grad_query: bfloat16 [16, 4096, 2048], P('dp', 'seq')
- grad_key: bfloat16 [16, 4096, 2048], P('dp', 'seq')
- grad_value: bfloat16 [16, 4096, 2048], P('dp', 'seq')
- grad_residue: float32 [16, 2048], P(None, 'seq')
- grad_lograte: float32 [16, 2048], P(None, 'seq')
- grad_skip: float32 [2048], P('seq')
The draws below stay inside these ranges and needn't reach their ends.
All inputs are finite; a program needn't handle non-finite values.
Results may differ from the reference program's by a relative error of at most 0.01.
Values may be sent and summed in bfloat16 or wider, within the bound.
A program may use at most 128 MiB of HBM per device.

```python
import math
import jax
import jax.numpy as jnp
from jax import lax

C = 2048
ORDER = 16
SEQ_LEN = 4096
BATCH = 16


def steps_of(stream_key, shape, pieces, low, top_value):
    gain = 1.0
    for dim, shards_of in pieces:
        steps = jax.random.uniform(jax.random.fold_in(jax.random.fold_in(stream_key, 6), dim), (shards_of,), jnp.float32, low / len(pieces), top_value / len(pieces))
        gain = gain * jnp.repeat(jnp.exp(steps), shape[dim] // shards_of).reshape((-1,) + (1,) * (len(shape) - 1 - dim))
    return gain


def normal_values(rng, extent, scale, reach, pieces=(), kind=jnp.bfloat16):
    entries = jax.random.normal(rng, extent, jnp.float32) * scale
    if len(pieces) > 0:
        entries = steps_of(rng, extent, pieces, -0.22, 0.18) * entries
    return jnp.clip(entries, min=-reach, max=reach).astype(kind)


def setup_inputs(seed: int = 0) -> dict:
    streams_of = jax.random.split(jax.random.key(seed), 8)
    return {
        "queries": normal_values(streams_of[0], (BATCH, SEQ_LEN, C), 1.0, 6.0, ((0, 16), (1, 32))),
        "key_branch": normal_values(streams_of[1], (BATCH, SEQ_LEN, C), 1.0, 6.0, ((0, 16), (1, 32))),
        "value_branch": normal_values(streams_of[2], (BATCH, SEQ_LEN, C), 1.0, 6.0, ((0, 16), (1, 32))),
        "cotangent": normal_values(streams_of[3], (BATCH, SEQ_LEN, C), 1.0, 6.0, ((0, 16), (1, 32))),
        "residues": normal_values(streams_of[4], (ORDER, C), (ORDER * SEQ_LEN // 4) ** -0.5, 0.046875, (), jnp.float32),
        "rates": jnp.clip(jnp.exp(jax.random.uniform(streams_of[5], (ORDER, C), jnp.float32, math.log(0.2), math.log(300.0))), 0.2, 300.0),
        "skip_gain": jnp.clip(jax.random.uniform(streams_of[6], (C,), jnp.float32, 0.5, 1.5), 0.5, 1.5),
    }


def rounded(values):
    return lax.optimization_barrier(values.astype(jnp.bfloat16)).astype(jnp.float32)


def reference(queries, key_branch, value_branch, cotangent, residues, rates, skip_gain):
    length = SEQ_LEN
    steps_f = jnp.arange(length, dtype=jnp.float32)
    decay = rates / jnp.float32(length)
    taps = jnp.zeros((length, residues.shape[1]), jnp.float32)
    for mode in range(residues.shape[0]):
        taps = taps + residues[mode][None, :] * jnp.exp(-decay[mode][None, :] * steps_f[:, None])
    filt = jnp.fft.rfft(taps, n=2 * length, axis=0)

    def one_seq(carry, items):
        lag_sum, skip_sum = carry
        query_s, key_s, value_s, cot_s = items
        key_f = key_s.astype(jnp.float32)
        value_f = value_s.astype(jnp.float32)
        prod_f = rounded(key_f * value_f)
        carr_f = rounded(cot_s.astype(jnp.float32) * query_s.astype(jnp.float32))
        spec_p = jnp.fft.rfft(prod_f, n=2 * length, axis=0)
        spec_c = jnp.fft.rfft(carr_f, n=2 * length, axis=0)
        conv = rounded(jnp.fft.irfft(spec_p * filt, n=2 * length, axis=0)[:length].astype(jnp.float32))
        back = rounded(jnp.fft.irfft(jnp.conj(filt) * spec_c, n=2 * length, axis=0)[:length].astype(jnp.float32))
        lagged = jnp.fft.irfft(spec_c * jnp.conj(spec_p), n=2 * length, axis=0)[:length].astype(jnp.float32)
        grad_q = (cot_s.astype(jnp.float32) * (conv + skip_gain[None, :] * prod_f)).astype(jnp.bfloat16)
        dz_full = back + skip_gain[None, :] * carr_f
        grad_k = (dz_full * value_f).astype(jnp.bfloat16)
        grad_v = (dz_full * key_f).astype(jnp.bfloat16)
        return (lag_sum + lagged, skip_sum + jnp.sum(carr_f * prod_f, axis=0)), (grad_q, grad_k, grad_v)

    init = (jnp.zeros((length, residues.shape[1]), jnp.float32), jnp.zeros((residues.shape[1],), jnp.float32))
    (lag_sum, skip_sum), (grad_query, grad_key, grad_value) = lax.scan(one_seq, init, (queries, key_branch, value_branch, cotangent))
    res_rows = []
    log_rows = []
    for mode in range(residues.shape[0]):
        weights = jnp.exp(-decay[mode][None, :] * steps_f[:, None])
        res_rows.append(jnp.sum(lag_sum * weights, axis=0))
        log_rows.append(-residues[mode] * decay[mode] * jnp.sum(lag_sum * weights * steps_f[:, None], axis=0))
    scale = jnp.float32(length)
    grad_residue = jnp.stack(res_rows) / scale
    grad_lograte = jnp.stack(log_rows) / scale
    grad_skip = skip_sum / scale
    return grad_query, grad_key, grad_value, grad_residue, grad_lograte, grad_skip
```

```python
import functools

import jax
import jax.numpy as jnp
import ml_dtypes
import numpy as np
from jax import lax
from jax.experimental import pallas as pl
from jax.experimental.pallas import tpu as pltpu
from jax.sharding import PartitionSpec as P

MESH = pl.DeviceIdType.MESH
f32 = jnp.float32
bf16 = jnp.bfloat16


def split_table(table):
    high = table.astype(ml_dtypes.bfloat16)
    low = (table - high.astype(np.float64)).astype(ml_dtypes.bfloat16)
    return high, low


def dft_tables(rows):
    odd = 2 * np.arange(rows)[:, None] + 1
    angle = np.pi / (2 * rows) * (odd * np.arange(rows)[None, :] % (4 * rows))
    forward = np.concatenate([np.cos(angle), -np.sin(angle)], axis=0)
    inverse = np.concatenate([np.cos(angle).T, -np.sin(angle).T], axis=1) / rows
    fwd = np.concatenate(split_table(forward), axis=1)
    inv = np.concatenate(split_table(inverse), axis=0)
    return fwd, inv


def main_kernel(
    rows,
    channels,
    groups,
    batch,
    q_hbm,
    k_hbm,
    v_hbm,
    o_hbm,
    res_ref,
    rates_ref,
    gain_ref,
    fwd_ref,
    inv_ref,
    y_hbm,
    dz_hbm,
    grad_ref,
    q_in,
    k_in,
    v_in,
    o_in,
    prod2,
    carr2,
    prod_f,
    carr_f,
    prod_w,
    carr_w,
    conv_s,
    back_s,
    lag_s,
    lag_w,
    up_tab,
    down_tab,
    gam_one,
    gam_eight,
    coef_t,
    coef_h,
    coef_k,
    y_out,
    dz_out,
    send_a,
    recv_a,
    send_b,
    recv_b,
    send_l,
    recv_l,
    send_g,
    recv_g,
    in_sem,
    out_sem,
    a_send,
    a_recv,
    b_send,
    b_recv,
    l_send,
    l_recv,
    g_send,
    g_recv,
):
    length = rows * groups
    inv_len = 1.0 / length
    wide = min(512, channels)
    mid = min(256, channels)
    chunks = channels // wide
    per_chunk = groups // chunks
    me = lax.axis_index("seq")
    me_b = lax.axis_index("dp")

    def seq_peer(step):
        return lax.rem(me + step, groups)

    def dp_peer(step):
        return lax.rem(me_b + step, batch)

    def lanes_of(index, size):
        return pl.ds(pl.multiple_of(index * size, size), size)

    def chunk_at(step):
        return lax.rem(me // per_chunk + step, chunks)

    def in_copies(step):
        lanes = lanes_of(chunk_at(step), wide)
        return [
            pltpu.make_async_copy(src.at[:, lanes], dst.at[:, lanes], in_sem.at[which, step])
            for which, (src, dst) in enumerate(
                ((k_hbm, k_in), (v_hbm, v_in), (o_hbm, o_in), (q_hbm, q_in))
            )
        ]

    for step in range(chunks):
        for copy in in_copies(step):
            copy.start()

    barrier = pltpu.get_barrier_semaphore()

    def greet_seq(step, _):
        pl.semaphore_signal(barrier, inc=1, device_id={"seq": seq_peer(step)}, device_id_type=MESH)
        return 0

    def greet_dp(step, _):
        pl.semaphore_signal(barrier, inc=1, device_id={"dp": dp_peer(step)}, device_id_type=MESH)
        return 0

    lax.fori_loop(1, groups, greet_seq, 0)
    lax.fori_loop(1, batch, greet_dp, 0)

    decay_all = rates_ref[...] * inv_len
    gam_one[...] = jnp.exp(-decay_all)
    sub = lax.broadcasted_iota(jnp.int32, (8, channels), 0).astype(f32)

    def table_body(n, _):
        rate = rates_ref[pl.ds(n, 1), :] * inv_len
        gam_eight[n] = jnp.exp(-8.0 * rate)
        coef_t[n] = res_ref[pl.ds(n, 1), :]
        up_tab[n] = jnp.exp(-rate * sub)
        down_tab[n] = jnp.exp(-rate * (8.0 - sub))
        return 0

    lax.fori_loop(0, 16, table_body, 0)

    lane = lax.broadcasted_iota(jnp.int32, (8, 128), 1)
    left = lane < 64

    def pack(block):
        top = block[0:8]
        low = block[8:16]
        return (
            jnp.where(left, top, pltpu.roll(low, 64, 1)),
            jnp.where(left, pltpu.roll(top, 64, 1), low),
        )

    def horner(up_refs, down_refs, lanes, width):
        gamma = gam_one[:, lanes]
        zero = jnp.zeros((16, width), f32)
        ups = len(up_refs)

        def body(i, carry):
            ups_in = [ref[pl.ds(pl.multiple_of(i * 8, 8), 8), lanes] for ref in up_refs]
            base = pl.multiple_of(rows - 8 - i * 8, 8)
            downs_in = [ref[pl.ds(base, 8), lanes] for ref in down_refs]
            totals = list(carry)
            for r in range(8):
                for which, block in enumerate(ups_in):
                    totals[which] = totals[which] * gamma + block[r : r + 1]
                for which, block in enumerate(downs_in):
                    totals[ups + which] = totals[ups + which] * gamma + block[7 - r : 8 - r]
            return tuple(totals)

        count = ups + len(down_refs)
        totals = lax.fori_loop(0, rows // 8, body, (zero,) * count, unroll=2)
        return [t * gamma for t in totals[:ups]] + list(totals[ups:])

    def send_a_copy(owner):
        return pltpu.make_async_remote_copy(
            src_ref=send_a.at[owner],
            dst_ref=recv_a.at[me],
            send_sem=a_send,
            recv_sem=a_recv,
            device_id={"seq": owner},
            device_id_type=MESH,
        )

    down_weight = (rows - lax.broadcasted_iota(jnp.int32, (rows, wide), 0)).astype(f32)
    up_weight = lax.broadcasted_iota(jnp.int32, (rows, wide), 0).astype(f32)

    for step in range(chunks):
        chunk = chunk_at(step)
        lanes = lanes_of(chunk, wide)
        for copy in in_copies(step):
            copy.wait()
        prod = (k_in[:, lanes].astype(f32) * v_in[:, lanes].astype(f32)).astype(bf16)
        carr = (o_in[:, lanes].astype(f32) * q_in[:, lanes].astype(f32)).astype(bf16)
        prod2[0:rows, lanes] = prod
        prod2[rows : 2 * rows, lanes] = prod
        carr2[0:rows, lanes] = carr
        carr2[rows : 2 * rows, lanes] = carr
        prod_32 = prod.astype(f32)
        carr_32 = carr.astype(f32)
        prod_f[:, lanes] = prod_32
        carr_f[:, lanes] = carr_32
        prod_w[:, lanes] = prod_32 * down_weight
        carr_w[:, lanes] = carr_32 * up_weight
        skip = jnp.sum(prod_32 * carr_32, axis=0, keepdims=True)
        state_p, state_c = horner([prod_f], [carr_f], lanes, wide)
        for part in range(wide // 128):
            cut = slice(part * 128, part * 128 + 128)
            pair = chunk * (wide // 128) + part
            for half, (p_tile, c_tile) in enumerate(zip(pack(state_p[:, cut]), pack(state_c[:, cut]))):
                send_a[2 * pair + half, 0:8, :] = p_tile
                send_a[2 * pair + half, 8:16, :] = c_tile
            row = skip[:, cut]
            send_a[2 * pair, 16:17, :] = row
            send_a[2 * pair + 1, 16:17, :] = pltpu.roll(row, 64, 1)
        if step == 0:
            pl.semaphore_wait(barrier, groups - 1 + batch - 1)

        def send_body(i, _):
            owner = chunk * per_chunk + lax.rem(me + i, per_chunk)

            @pl.when(owner != me)
            def _():
                send_a_copy(owner).start()

            return 0

        lax.fori_loop(0, per_chunk, send_body, 0)
    recv_a[me] = send_a[me]

    def synth(coef_ref, table_ref, lanes, width, ascending):
        def body(n, accs):
            accs = list(accs)
            wave = table_ref[n, :, lanes] * coef_ref[n, :, lanes]
            ratio = jnp.broadcast_to(gam_eight[n, :, lanes], (8, width))
            blocks = range(rows // 8) if ascending else range(rows // 8 - 1, -1, -1)
            for order, block in enumerate(blocks):
                accs[block] = accs[block] + wave
                if order < rows // 8 - 1:
                    wave = wave * ratio
            return tuple(accs)

        zero = jnp.zeros((8, width), f32)
        accs = lax.fori_loop(0, 16, body, (zero,) * (rows // 8), unroll=2)
        return jnp.concatenate(accs, axis=0)

    def dot(a, b):
        return jnp.dot(a, b, preferred_element_type=f32)

    def spectrum_body(j, _):
        lanes = lanes_of(j, mid)
        taps = synth(coef_t, up_tab, lanes, mid, True)
        high = taps.astype(bf16)
        low = (taps - high.astype(f32)).astype(bf16)
        table = fwd_ref[...]
        filt = dot(table, jnp.concatenate([high, high], axis=0)) + dot(table[:, :rows], low)
        spec_p = dot(table, prod2[:, lanes])
        spec_c = dot(table, carr2[:, lanes])
        fr, fi = filt[:rows], filt[rows:]
        pr, pi = spec_p[:rows], spec_p[rows:]
        cr, ci = spec_c[:rows], spec_c[rows:]
        inverse = inv_ref[...]

        def back_to_rows(real, imag):
            spec = jnp.concatenate([real.astype(bf16), imag.astype(bf16)], axis=0)
            both = dot(inverse, spec)
            return both[:rows] + both[rows:]

        conv_s[:, lanes] = back_to_rows(pr * fr - pi * fi, pr * fi + pi * fr)
        back_s[:, lanes] = back_to_rows(cr * fr + ci * fi, ci * fr - cr * fi)
        lag = back_to_rows(cr * pr + ci * pi, ci * pr - cr * pi)
        lag_s[:, lanes] = lag
        lag_w[:, lanes] = lag * up_weight[:, :mid]
        return 0

    lax.fori_loop(0, channels // mid, spectrum_body, 0)

    def wait_bytes(ref, sem, count):
        block = ref.at[pl.ds(0, count)]
        pltpu.make_async_copy(block, block, sem).wait()

    wait_bytes(recv_a, a_recv, groups - 1)
    own_lanes = lanes_of(me // 2, 128)
    is_left = lax.rem(me, 2) == 0

    def own_pack(block):
        first, second = pack(block)
        return jnp.where(is_left, first, second)

    own_decay = own_pack(rates_ref[:, own_lanes]) * inv_len
    own_res = own_pack(res_ref[:, own_lanes])
    span = jnp.exp(-own_decay * float(rows))
    zero = jnp.zeros((8, 128), f32)

    def up_scan(i, carry):
        state, slope, total, moment = carry
        p_in = recv_a[i, 0:8, :]
        c_in = recv_a[i, 8:16, :]
        send_b[i, 0:8, :] = state
        total = total + c_in * state
        moment = moment + c_in * slope
        slope = span * (slope + state)
        state = span * state + p_in
        return state, slope, total, moment

    _, _, total, moment = lax.fori_loop(0, groups, up_scan, (zero, zero, zero, zero), unroll=4)

    def down_scan(i, state):
        at = groups - 1 - i
        send_b[at, 8:16, :] = state
        return span * state + recv_a[at, 8:16, :]

    lax.fori_loop(0, groups, down_scan, zero, unroll=4)

    def send_b_body(step, _):
        owner = seq_peer(step)
        pltpu.make_async_remote_copy(
            src_ref=send_b.at[owner],
            dst_ref=recv_b.at[me],
            send_sem=b_send,
            recv_sem=b_recv,
            device_id={"seq": owner},
            device_id_type=MESH,
        ).start()
        return 0

    lax.fori_loop(1, groups, send_b_body, 0)
    recv_b[me] = send_b[me]

    def skip_body(i, acc):
        return acc + recv_a[i, 16:17, :]

    skip_sum = lax.fori_loop(0, groups, skip_body, jnp.zeros((1, 128), f32))

    def moments_body(j, _):
        lanes = lanes_of(j, mid)
        slope_p, slope_c, lag_0, lag_1 = horner([prod_w], [carr_w, lag_s, lag_w], lanes, mid)
        for part in range(mid // 128):
            cut = slice(part * 128, part * 128 + 128)
            pair = j * (mid // 128) + part
            tiles = [pack(x[:, cut]) for x in (slope_p, slope_c, lag_0, lag_1)]
            for half in range(2):
                send_l[2 * pair + half, 0] = jnp.concatenate(
                    [tiles[0][half], tiles[1][half]], axis=0
                ).astype(bf16)
                send_l[2 * pair + half, 1] = jnp.concatenate(
                    [tiles[2][half], tiles[3][half]], axis=0
                ).astype(bf16)
        return 0

    lax.fori_loop(0, channels // mid, moments_body, 0)

    def send_l_body(step, _):
        owner = seq_peer(step)
        pltpu.make_async_remote_copy(
            src_ref=send_l.at[owner],
            dst_ref=recv_l.at[me],
            send_sem=l_send,
            recv_sem=l_recv,
            device_id={"seq": owner},
            device_id_type=MESH,
        ).start()
        return 0

    lax.fori_loop(1, groups, send_l_body, 0)
    recv_l[me] = send_l[me]

    wait_bytes(recv_b, b_recv, groups - 1)

    def unpack_body(j, _):
        lanes = lanes_of(j, 128)
        res = res_ref[:, lanes]
        for half, coef in ((0, coef_h), (8, coef_k)):
            first = recv_b[2 * j, half : half + 8, :]
            second = recv_b[2 * j + 1, half : half + 8, :]
            low = res[0:8] * jnp.where(left, first, pltpu.roll(second, 64, 1))
            high = res[8:16] * jnp.where(left, pltpu.roll(first, 64, 1), second)
            for row in range(8):
                coef[row, :, lanes] = low[row : row + 1]
                coef[row + 8, :, lanes] = high[row : row + 1]
        return 0

    lax.fori_loop(0, channels // 128, unpack_body, 0)

    def out_copies(j):
        lanes = lanes_of(j, mid)
        return [
            pltpu.make_async_copy(src.at[:, lanes], dst.at[:, lanes], out_sem.at[which])
            for which, (src, dst) in enumerate(((y_out, y_hbm), (dz_out, dz_hbm)))
        ]

    def final_body(j, _):
        for part in range(mid // 128):
            lanes = lanes_of(j * (mid // 128) + part, 128)
            conv = conv_s[:, lanes] + synth(coef_h, up_tab, lanes, 128, True)
            back = back_s[:, lanes] + synth(coef_k, down_tab, lanes, 128, False)
            gain = gain_ref[:, lanes]
            y_out[:, lanes] = conv.astype(bf16).astype(f32) + gain * prod_f[:, lanes]
            dz_out[:, lanes] = back.astype(bf16).astype(f32) + gain * carr_f[:, lanes]
        for copy in out_copies(j):
            copy.start()
        return 0

    steps = channels // mid
    early = steps // 2
    lax.fori_loop(0, early, final_body, 0)

    wait_bytes(recv_l, l_recv, groups - 1)

    def combine_body(i, carry):
        grad_0, grad_1 = carry
        slopes = recv_l[i, 0].astype(f32)
        lags = recv_l[i, 1].astype(f32)
        grad_0 = grad_0 + lags[0:8]
        grad_1 = grad_1 + lags[8:16]
        grad_1 = grad_1 + slopes[8:16] * send_b[i, 0:8, :] + slopes[0:8] * send_b[i, 8:16, :]
        return grad_0, grad_1

    grad_0, grad_1 = lax.fori_loop(
        0, groups, combine_body, (total, float(rows) * moment), unroll=4
    )
    send_g[0:8, :] = grad_0 * inv_len
    send_g[8:16, :] = -own_res * own_decay * grad_1 * inv_len
    send_g[16:17, :] = skip_sum * inv_len

    def send_g_body(step, _):
        pltpu.make_async_remote_copy(
            src_ref=send_g,
            dst_ref=recv_g.at[me_b],
            send_sem=g_send,
            recv_sem=g_recv,
            device_id={"dp": dp_peer(step)},
            device_id_type=MESH,
        ).start()
        return 0

    lax.fori_loop(1, batch, send_g_body, 0)
    recv_g[me_b] = send_g[...]
    lax.fori_loop(early, steps, final_body, 0)
    wait_bytes(recv_g, g_recv, batch - 1)

    def total_body(i, acc):
        return acc + recv_g[i]

    grad_ref[0:17, :] = lax.fori_loop(0, batch, total_body, jnp.zeros((17, 128), f32))

    wait_bytes(send_a, a_send, groups - 1)
    wait_bytes(send_b, b_send, groups - 1)
    wait_bytes(send_l, l_send, groups - 1)
    wait_bytes(recv_g, g_send, batch - 1)

    def drain(j, _):
        for copy in out_copies(j):
            copy.wait()
        return 0

    lax.fori_loop(0, steps, drain, 0)


def gate_kernel(cot, key, value, y, dz, grads, grad_q, grad_k, grad_v, grad_r, grad_l, grad_s):
    dz_now = dz[...]
    grad_q[...] = (cot[...].astype(f32) * y[...]).astype(bf16)
    grad_k[...] = (dz_now * value[...].astype(f32)).astype(bf16)
    grad_v[...] = (dz_now * key[...].astype(f32)).astype(bf16)

    @pl.when(pl.program_id(0) == 0)
    def _():
        for start, out in ((0, grad_r), (8, grad_l)):
            tile = grads[start : start + 8, :]
            out[0:8, :] = tile[:, 0:64]
            out[8:16, :] = pltpu.roll(tile, 64, 1)[:, 0:64]
        grad_s[...] = grads[16:17, 0:64]


def shards(queries, key_branch, value_branch, cotangent, residues, rates, skip_gain):
    groups = lax.axis_size("seq")
    batch = lax.axis_size("dp")
    rows, channels = queries.shape[1:]
    fwd, inv = dft_tables(rows)
    q, k, v, o = (x[0] for x in (queries, key_branch, value_branch, cotangent))
    hbm = pl.BlockSpec(memory_space=pl.ANY)
    vmem = pl.BlockSpec(memory_space=pltpu.VMEM)
    big = pltpu.VMEM((rows, channels), f32)
    half = pltpu.VMEM((rows, channels), bf16)
    dma = pltpu.SemaphoreType.DMA
    chunks = channels // min(512, channels)
    y, dz, grads = pl.pallas_call(
        functools.partial(main_kernel, rows, channels, groups, batch),
        out_shape=[
            jax.ShapeDtypeStruct((rows, channels), f32),
            jax.ShapeDtypeStruct((rows, channels), f32),
            jax.ShapeDtypeStruct((24, 128), f32),
        ],
        in_specs=[hbm] * 4 + [vmem] * 5,
        out_specs=[hbm, hbm, vmem],
        scratch_shapes=[half] * 4
        + [pltpu.VMEM((2 * rows, channels), bf16)] * 2
        + [big] * 8
        + [pltpu.VMEM((16, 8, channels), f32)] * 2
        + [pltpu.VMEM((16, channels), f32)]
        + [pltpu.VMEM((16, 1, channels), f32)] * 4
        + [big] * 2
        + [pltpu.VMEM((groups, 17, 128), f32)] * 2
        + [pltpu.VMEM((groups, 16, 128), f32)] * 2
        + [pltpu.VMEM((groups, 2, 16, 128), bf16)] * 2
        + [pltpu.VMEM((17, 128), f32), pltpu.VMEM((batch, 17, 128), f32)]
        + [dma((4, chunks)), dma((2,))]
        + [dma] * 8,
        compiler_params=pltpu.CompilerParams(
            collective_id=0, has_side_effects=True, vmem_limit_bytes=48 * 2**20
        ),
        name="hyena_main",
    )(q, k, v, o, residues, rates, skip_gain[None, :], jnp.asarray(fwd), jnp.asarray(inv))
    tile = min(32, rows)
    rowed = pl.BlockSpec((tile, channels), lambda i: (i, 0))

    def whole(*shape):
        return pl.BlockSpec(shape, lambda i: (0, 0))

    wide16 = jax.ShapeDtypeStruct((rows, channels), bf16)
    gq, gk, gv, gr, gl, gs = pl.pallas_call(
        gate_kernel,
        grid=(rows // tile,),
        out_shape=[wide16] * 3
        + [jax.ShapeDtypeStruct((16, 64), f32)] * 2
        + [jax.ShapeDtypeStruct((1, 64), f32)],
        in_specs=[rowed] * 5 + [whole(24, 128)],
        out_specs=[rowed] * 3 + [whole(16, 64), whole(16, 64), whole(1, 64)],
        name="hyena_gate",
    )(o, k, v, y, dz, grads)
    return gq[None], gk[None], gv[None], gr, gl, gs[0]


def solution(mesh):
    row_spec = P("dp", "seq", None)
    return jax.shard_map(
        shards,
        mesh=mesh,
        in_specs=(row_spec,) * 4 + (P(),) * 3,
        out_specs=(row_spec,) * 3 + (P(None, "seq"), P(None, "seq"), P("seq")),
        check_vma=False,
    )
```

```python
import functools

import jax
import jax.numpy as jnp
import ml_dtypes
import numpy as np
from jax import lax
from jax.experimental import pallas as pl
from jax.experimental.pallas import tpu as pltpu
from jax.sharding import PartitionSpec as P

MESH = pl.DeviceIdType.MESH
f32 = jnp.float32
bf16 = jnp.bfloat16


def split_table(table):
    high = table.astype(ml_dtypes.bfloat16)
    low = (table - high.astype(np.float64)).astype(ml_dtypes.bfloat16)
    return high, low


def dft_tables(rows):
    odd = 2 * np.arange(rows)[:, None] + 1
    angle = np.pi / (2 * rows) * (odd * np.arange(rows)[None, :] % (4 * rows))
    forward = np.concatenate([np.cos(angle), -np.sin(angle)], axis=0)
    inverse = np.concatenate([np.cos(angle).T, -np.sin(angle).T], axis=1) / rows
    return forward, inverse


def stacked_tables(rows, sub_rows):
    forward, inverse = dft_tables(rows)
    sub_fwd, sub_inv = dft_tables(sub_rows)
    parts = rows // sub_rows
    blocks = np.zeros((2, sub_rows, parts, parts, sub_rows))
    for part in range(parts):
        blocks[:, :, part, part, :] = sub_fwd.reshape(2, sub_rows, sub_rows)
    blocks = blocks.transpose(0, 2, 1, 3, 4).reshape(2 * rows, rows)
    fwd = np.concatenate(split_table(forward), axis=1)
    inv = np.concatenate(split_table(inverse), axis=0)
    fwd_sub = np.concatenate(split_table(blocks), axis=1)
    inv_sub = np.concatenate(split_table(sub_inv), axis=0)
    return fwd, inv, fwd_sub, inv_sub


def main_kernel(
    rows,
    channels,
    groups,
    batch,
    q_hbm,
    k_hbm,
    v_hbm,
    o_hbm,
    res_hbm,
    rates_hbm,
    gain_hbm,
    fwd_hbm,
    inv_hbm,
    fsub_hbm,
    isub_hbm,
    y_hbm,
    dz_hbm,
    grad_ref,
    res_ref,
    rates_ref,
    gain_ref,
    fwd_ref,
    inv_ref,
    fsub_ref,
    isub_ref,
    q_in,
    k_in,
    v_in,
    o_in,
    prod2,
    carr2,
    prod_f,
    carr_f,
    prod_w,
    carr_w,
    conv_s,
    back_s,
    lag_s,
    lag_w,
    up_tab,
    down_tab,
    gam_one,
    gam_sub,
    sub_s,
    sub_b,
    sub_s1,
    sub_b1,
    gam_eight,
    coef_t,
    coef_h,
    coef_k,
    y_out,
    dz_out,
    send_a,
    recv_a,
    send_b,
    recv_b,
    send_l,
    recv_l,
    send_g,
    recv_g,
    in_sem,
    small_sem,
    out_sem,
    a_send,
    a_recv,
    b_send,
    b_recv,
    l_send,
    l_recv,
    g_send,
    g_recv,
):
    length = rows * groups
    inv_len = 1.0 / length
    sub_rows = isub_ref.shape[0] // 2
    parts = rows // sub_rows
    wide = min(512, channels)
    mid = min(256, channels)
    chunks = channels // wide
    per_chunk = groups // chunks
    me = lax.axis_index("seq")
    me_b = lax.axis_index("dp")

    def seq_peer(step):
        return lax.rem(me + step, groups)

    def dp_peer(step):
        return lax.rem(me_b + step, batch)

    def lanes_of(index, size):
        return pl.ds(pl.multiple_of(index * size, size), size)

    def chunk_at(step):
        return lax.rem(me // per_chunk + step, chunks)

    def in_copies(step):
        lanes = lanes_of(chunk_at(step), wide)
        return [
            pltpu.make_async_copy(src.at[:, lanes], dst.at[:, lanes], in_sem.at[which, step])
            for which, (src, dst) in enumerate(
                ((k_hbm, k_in), (v_hbm, v_in), (o_hbm, o_in), (q_hbm, q_in))
            )
        ]

    small = [
        pltpu.make_async_copy(src, dst, small_sem.at[which])
        for which, (src, dst) in enumerate(
            (
                (rates_hbm, rates_ref),
                (res_hbm, res_ref),
                (gain_hbm, gain_ref),
                (fwd_hbm, fwd_ref),
                (inv_hbm, inv_ref),
                (fsub_hbm, fsub_ref),
                (isub_hbm, isub_ref),
            )
        )
    ]
    for copy in small[:2]:
        copy.start()
    for step in range(chunks):
        for copy in in_copies(step):
            copy.start()
    for copy in small[2:]:
        copy.start()

    barrier = pltpu.get_barrier_semaphore()

    def greet_seq(step, _):
        pl.semaphore_signal(barrier, inc=1, device_id={"seq": seq_peer(step)}, device_id_type=MESH)
        return 0

    def greet_dp(step, _):
        pl.semaphore_signal(barrier, inc=1, device_id={"dp": dp_peer(step)}, device_id_type=MESH)
        return 0

    lax.fori_loop(1, groups, greet_seq, 0)
    lax.fori_loop(1, batch, greet_dp, 0)

    for copy in small[:2]:
        copy.wait()
    decay_all = rates_ref[...] * inv_len
    gam_one[...] = jnp.exp(-decay_all)
    gam_sub[...] = jnp.exp(-float(sub_rows) * decay_all)
    sub = lax.broadcasted_iota(jnp.int32, (8, channels), 0).astype(f32)

    def table_body(n, _):
        rate = rates_ref[pl.ds(n, 1), :] * inv_len
        gam_eight[n] = jnp.exp(-8.0 * rate)
        coef_t[n] = res_ref[pl.ds(n, 1), :]
        up_tab[n] = jnp.exp(-rate * sub)
        down_tab[n] = jnp.exp(-rate * (8.0 - sub))
        return 0

    lax.fori_loop(0, 16, table_body, 0)

    lane = lax.broadcasted_iota(jnp.int32, (8, 128), 1)
    left = lane < 64

    def pack(block):
        top = block[0:8]
        low = block[8:16]
        return (
            jnp.where(left, top, pltpu.roll(low, 64, 1)),
            jnp.where(left, pltpu.roll(top, 64, 1), low),
        )

    def horner(up_refs, down_refs, base, lanes, width):
        gamma = gam_one[:, lanes]
        totals = [jnp.zeros((16, width), f32)] * (len(up_refs) + len(down_refs))
        ups = len(up_refs)
        for i in range(sub_rows // 8):
            ups_in = [ref[pl.ds(pl.multiple_of(base + i * 8, 8), 8), lanes] for ref in up_refs]
            low = pl.multiple_of(base + sub_rows - 8 - i * 8, 8)
            downs_in = [ref[pl.ds(low, 8), lanes] for ref in down_refs]
            for r in range(8):
                for which, block in enumerate(ups_in):
                    totals[which] = totals[which] * gamma + block[r : r + 1]
                for which, block in enumerate(downs_in):
                    totals[ups + which] = totals[ups + which] * gamma + block[7 - r : 8 - r]
        return [t * gamma for t in totals[:ups]] + totals[ups:]

    def send_a_copy(owner):
        return pltpu.make_async_remote_copy(
            src_ref=send_a.at[owner],
            dst_ref=recv_a.at[me],
            send_sem=a_send,
            recv_sem=a_recv,
            device_id={"seq": owner},
            device_id_type=MESH,
        )

    local = lax.rem(lax.broadcasted_iota(jnp.int32, (rows, wide), 0), sub_rows)
    down_weight = (sub_rows - local).astype(f32)
    up_weight = local.astype(f32)

    for step in range(chunks):
        chunk = chunk_at(step)
        lanes = lanes_of(chunk, wide)
        for copy in in_copies(step):
            copy.wait()
        prod = (k_in[:, lanes].astype(f32) * v_in[:, lanes].astype(f32)).astype(bf16)
        carr = (o_in[:, lanes].astype(f32) * q_in[:, lanes].astype(f32)).astype(bf16)
        prod2[0:rows, lanes] = prod
        prod2[rows : 2 * rows, lanes] = prod
        carr2[0:rows, lanes] = carr
        carr2[rows : 2 * rows, lanes] = carr
        prod_32 = prod.astype(f32)
        carr_32 = carr.astype(f32)
        prod_f[:, lanes] = prod_32
        carr_f[:, lanes] = carr_32
        prod_w[:, lanes] = prod_32 * down_weight
        carr_w[:, lanes] = carr_32 * up_weight
        skip = jnp.sum(prod_32 * carr_32, axis=0, keepdims=True)

        def state_body(part, _):
            base = pl.multiple_of(part * sub_rows, sub_rows)
            sub_s[part, :, lanes], sub_b[part, :, lanes] = horner([prod_f], [carr_f], base, lanes, wide)
            return 0

        lax.fori_loop(0, parts, state_body, 0)
        ratio = gam_sub[:, lanes]
        state_p = sub_s[0, :, lanes]
        state_c = sub_b[parts - 1, :, lanes]
        for part in range(1, parts):
            state_p = state_p * ratio + sub_s[part, :, lanes]
            state_c = state_c * ratio + sub_b[parts - 1 - part, :, lanes]
        for part in range(wide // 128):
            cut = slice(part * 128, part * 128 + 128)
            pair = chunk * (wide // 128) + part
            for half, (p_tile, c_tile) in enumerate(zip(pack(state_p[:, cut]), pack(state_c[:, cut]))):
                send_a[2 * pair + half, 0:8, :] = p_tile
                send_a[2 * pair + half, 8:16, :] = c_tile
            row = skip[:, cut]
            send_a[2 * pair, 16:17, :] = row
            send_a[2 * pair + 1, 16:17, :] = pltpu.roll(row, 64, 1)
        if step == 0:
            pl.semaphore_wait(barrier, groups - 1 + batch - 1)

        def send_body(i, _):
            owner = chunk * per_chunk + lax.rem(me + i, per_chunk)

            @pl.when(owner != me)
            def _():
                send_a_copy(owner).start()

            return 0

        lax.fori_loop(0, per_chunk, send_body, 0)
    recv_a[me] = send_a[me]

    def synth(terms, lanes):
        count = rows // 8
        zero = jnp.zeros((8, 128), f32)

        def body(n, accs):
            accs = [list(acc) for acc in accs]
            ratio = jnp.broadcast_to(gam_eight[n, :, lanes], (8, 128))
            waves = [table[n, :, lanes] * coef[n, :, lanes] for coef, table, _ in terms]
            for order in range(count):
                for which, (_, _, ascending) in enumerate(terms):
                    block = order if ascending else count - 1 - order
                    accs[which][block] = accs[which][block] + waves[which]
                    if order < count - 1:
                        waves[which] = waves[which] * ratio
            return tuple(tuple(acc) for acc in accs)

        accs = lax.fori_loop(0, 16, body, ((zero,) * count,) * len(terms), unroll=4)
        return [jnp.concatenate(acc, axis=0) for acc in accs]

    def dot(a, b):
        return jnp.dot(a, b, preferred_element_type=f32)

    for copy in small[2:]:
        copy.wait()

    def lag_body(j, _):
        lanes = lanes_of(j, mid)
        table = fsub_ref[...]
        spec_p = dot(table, prod2[:, lanes])
        spec_c = dot(table, carr2[:, lanes])
        real = jnp.zeros((sub_rows, mid), f32)
        imag = jnp.zeros((sub_rows, mid), f32)
        for part in range(parts):
            lo = part * sub_rows
            pr, pi = spec_p[lo : lo + sub_rows], spec_p[rows + lo : rows + lo + sub_rows]
            cr, ci = spec_c[lo : lo + sub_rows], spec_c[rows + lo : rows + lo + sub_rows]
            real = real + (cr * pr + ci * pi)
            imag = imag + (ci * pr - cr * pi)
        both = dot(isub_ref[...], jnp.concatenate([real.astype(bf16), imag.astype(bf16)], axis=0))
        lag = both[:sub_rows] + both[sub_rows:]
        lag_s[:, lanes] = lag
        lag_w[:, lanes] = lag * up_weight[:sub_rows, :mid]
        return 0

    lax.fori_loop(0, channels // mid, lag_body, 0)

    def moments_body(j, _):
        lanes = lanes_of(j, wide)

        def slope_body(part, _):
            base = pl.multiple_of(part * sub_rows, sub_rows)
            sub_s1[part, :, lanes], sub_b1[part, :, lanes] = horner([prod_w], [carr_w], base, lanes, wide)
            return 0

        lax.fori_loop(0, parts, slope_body, 0)
        lag_0, lag_1 = horner([], [lag_s, lag_w], 0, lanes, wide)
        for part in range(wide // 128):
            cut = slice(part * 128, part * 128 + 128)
            pair = j * (wide // 128) + part
            own = lanes_of(pair, 128)
            ratio = gam_sub[:, own]
            total_0, total_1 = lag_0[:, cut], lag_1[:, cut]
            state, slope = sub_s[0, :, own], sub_s1[0, :, own]
            for q in range(1, parts):
                c_state = sub_b[q, :, own]
                total_0 = total_0 + c_state * state
                total_1 = total_1 + sub_b1[q, :, own] * state + c_state * slope
                slope = ratio * (slope + float(sub_rows) * state) + sub_s1[q, :, own]
                state = ratio * state + sub_s[q, :, own]
            c_slope = sub_b1[parts - 1, :, own]
            c_state = sub_b[parts - 1, :, own]
            for q in range(parts - 2, -1, -1):
                c_slope = ratio * (c_slope + float(sub_rows) * c_state) + sub_b1[q, :, own]
                c_state = ratio * c_state + sub_b[q, :, own]
            tiles = [pack(x) for x in (slope, c_slope, total_0, total_1)]
            for half in range(2):
                send_l[2 * pair + half, 0] = jnp.concatenate(
                    [tiles[0][half], tiles[1][half]], axis=0
                ).astype(bf16)
                send_l[2 * pair + half, 1] = jnp.concatenate(
                    [tiles[2][half], tiles[3][half]], axis=0
                ).astype(bf16)
        return 0

    lax.fori_loop(0, channels // wide, moments_body, 0)

    def send_l_body(step, _):
        owner = seq_peer(step)
        pltpu.make_async_remote_copy(
            src_ref=send_l.at[owner],
            dst_ref=recv_l.at[me],
            send_sem=l_send,
            recv_sem=l_recv,
            device_id={"seq": owner},
            device_id_type=MESH,
        ).start()
        return 0

    lax.fori_loop(1, groups, send_l_body, 0)
    recv_l[me] = send_l[me]

    def wait_bytes(ref, sem, count):
        block = ref.at[pl.ds(0, count)]
        pltpu.make_async_copy(block, block, sem).wait()

    wait_bytes(recv_a, a_recv, groups - 1)
    own_lanes = lanes_of(me // 2, 128)
    is_left = lax.rem(me, 2) == 0

    def own_pack(block):
        first, second = pack(block)
        return jnp.where(is_left, first, second)

    own_decay = own_pack(rates_ref[:, own_lanes]) * inv_len
    own_res = own_pack(res_ref[:, own_lanes])
    span = jnp.exp(-own_decay * float(rows))
    zero = jnp.zeros((8, 128), f32)

    def up_scan(i, carry):
        state, slope, total, moment = carry
        p_in = recv_a[i, 0:8, :]
        c_in = recv_a[i, 8:16, :]
        send_b[i, 0:8, :] = state
        total = total + c_in * state
        moment = moment + c_in * slope
        slope = span * (slope + state)
        state = span * state + p_in
        return state, slope, total, moment

    _, _, total, moment = lax.fori_loop(0, groups, up_scan, (zero, zero, zero, zero), unroll=4)

    def down_scan(i, state):
        at = groups - 1 - i
        send_b[at, 8:16, :] = state
        return span * state + recv_a[at, 8:16, :]

    lax.fori_loop(0, groups, down_scan, zero, unroll=4)

    def send_b_body(step, _):
        owner = seq_peer(step)
        pltpu.make_async_remote_copy(
            src_ref=send_b.at[owner],
            dst_ref=recv_b.at[me],
            send_sem=b_send,
            recv_sem=b_recv,
            device_id={"seq": owner},
            device_id_type=MESH,
        ).start()
        return 0

    lax.fori_loop(1, groups, send_b_body, 0)
    recv_b[me] = send_b[me]

    def skip_body(i, acc):
        return acc + recv_a[i, 16:17, :]

    skip_sum = lax.fori_loop(0, groups, skip_body, jnp.zeros((1, 128), f32))

    def conv_body(j, _):
        lanes = lanes_of(j, mid)
        taps = jnp.concatenate(
            [
                synth([(coef_t, up_tab, True)], lanes_of(j * (mid // 128) + part, 128))[0]
                for part in range(mid // 128)
            ],
            axis=1,
        )
        high = taps.astype(bf16)
        low = (taps - high.astype(f32)).astype(bf16)
        table = fwd_ref[...]
        filt = dot(table, jnp.concatenate([high, high], axis=0)) + dot(table[:, :rows], low)
        spec_p = dot(table, prod2[:, lanes])
        spec_c = dot(table, carr2[:, lanes])
        fr, fi = filt[:rows], filt[rows:]
        pr, pi = spec_p[:rows], spec_p[rows:]
        cr, ci = spec_c[:rows], spec_c[rows:]
        inverse = inv_ref[...]

        def back_to_rows(real, imag):
            spec = jnp.concatenate([real.astype(bf16), imag.astype(bf16)], axis=0)
            both = dot(inverse, spec)
            return both[:rows] + both[rows:]

        conv_s[:, lanes] = back_to_rows(pr * fr - pi * fi, pr * fi + pi * fr)
        back_s[:, lanes] = back_to_rows(cr * fr + ci * fi, ci * fr - cr * fi)
        return 0

    lax.fori_loop(0, channels // mid, conv_body, 0)

    wait_bytes(recv_b, b_recv, groups - 1)

    def unpack_body(j, _):
        lanes = lanes_of(j, 128)
        res = res_ref[:, lanes]
        for half, coef in ((0, coef_h), (8, coef_k)):
            first = recv_b[2 * j, half : half + 8, :]
            second = recv_b[2 * j + 1, half : half + 8, :]
            low = res[0:8] * jnp.where(left, first, pltpu.roll(second, 64, 1))
            high = res[8:16] * jnp.where(left, pltpu.roll(first, 64, 1), second)
            for row in range(8):
                coef[row, :, lanes] = low[row : row + 1]
                coef[row + 8, :, lanes] = high[row : row + 1]
        return 0

    lax.fori_loop(0, channels // 128, unpack_body, 0)

    def out_copies(j):
        lanes = lanes_of(j, mid)
        return [
            pltpu.make_async_copy(src.at[:, lanes], dst.at[:, lanes], out_sem.at[which])
            for which, (src, dst) in enumerate(((y_out, y_hbm), (dz_out, dz_hbm)))
        ]

    def final_body(j, _):
        for part in range(mid // 128):
            lanes = lanes_of(j * (mid // 128) + part, 128)
            far = synth([(coef_h, up_tab, True), (coef_k, down_tab, False)], lanes)
            conv = conv_s[:, lanes] + far[0]
            back = back_s[:, lanes] + far[1]
            gain = gain_ref[:, lanes]
            y_out[:, lanes] = (conv.astype(bf16).astype(f32) + gain * prod_f[:, lanes]).astype(bf16)
            dz_out[:, lanes] = (back.astype(bf16).astype(f32) + gain * carr_f[:, lanes]).astype(bf16)
        for copy in out_copies(j):
            copy.start()
        return 0

    steps = channels // mid
    early = steps // 2
    lax.fori_loop(0, early, final_body, 0)

    wait_bytes(recv_l, l_recv, groups - 1)

    def combine_body(i, carry):
        grad_0, grad_1 = carry
        slopes = recv_l[i, 0].astype(f32)
        lags = recv_l[i, 1].astype(f32)
        grad_0 = grad_0 + lags[0:8]
        grad_1 = grad_1 + lags[8:16]
        grad_1 = grad_1 + slopes[8:16] * send_b[i, 0:8, :] + slopes[0:8] * send_b[i, 8:16, :]
        return grad_0, grad_1

    grad_0, grad_1 = lax.fori_loop(
        0, groups, combine_body, (total, float(rows) * moment), unroll=4
    )
    send_g[0:8, :] = grad_0 * inv_len
    send_g[8:16, :] = -own_res * own_decay * grad_1 * inv_len
    send_g[16:17, :] = skip_sum * inv_len

    def send_g_body(step, _):
        pltpu.make_async_remote_copy(
            src_ref=send_g,
            dst_ref=recv_g.at[me_b],
            send_sem=g_send,
            recv_sem=g_recv,
            device_id={"dp": dp_peer(step)},
            device_id_type=MESH,
        ).start()
        return 0

    lax.fori_loop(1, batch, send_g_body, 0)
    recv_g[me_b] = send_g[...]
    lax.fori_loop(early, steps, final_body, 0)
    wait_bytes(recv_g, g_recv, batch - 1)

    def total_body(i, acc):
        return acc + recv_g[i]

    grad_ref[0:17, :] = lax.fori_loop(0, batch, total_body, jnp.zeros((17, 128), f32))

    wait_bytes(send_a, a_send, groups - 1)
    wait_bytes(send_b, b_send, groups - 1)
    wait_bytes(send_l, l_send, groups - 1)
    wait_bytes(recv_g, g_send, batch - 1)

    def drain(j, _):
        for copy in out_copies(j):
            copy.wait()
        return 0

    lax.fori_loop(0, steps, drain, 0)


def gate_kernel(cot, key, value, y, dz, grads, grad_q, grad_k, grad_v, grad_r, grad_l, grad_s):
    dz_now = dz[...].astype(f32)
    grad_q[...] = (cot[...].astype(f32) * y[...].astype(f32)).astype(bf16)
    grad_k[...] = (dz_now * value[...].astype(f32)).astype(bf16)
    grad_v[...] = (dz_now * key[...].astype(f32)).astype(bf16)

    @pl.when(pl.program_id(0) == 0)
    def _():
        for start, out in ((0, grad_r), (8, grad_l)):
            tile = grads[start : start + 8, :]
            out[0:8, :] = tile[:, 0:64]
            out[8:16, :] = pltpu.roll(tile, 64, 1)[:, 0:64]
        grad_s[...] = grads[16:17, 0:64]


def shards(queries, key_branch, value_branch, cotangent, residues, rates, skip_gain):
    groups = lax.axis_size("seq")
    batch = lax.axis_size("dp")
    rows, channels = queries.shape[1:]
    sub_rows = 32
    tables = [jnp.asarray(table) for table in stacked_tables(rows, sub_rows)]
    q, k, v, o = (x[0] for x in (queries, key_branch, value_branch, cotangent))
    hbm = pl.BlockSpec(memory_space=pltpu.HBM)
    big = pltpu.VMEM((rows, channels), f32)
    half = pltpu.VMEM((rows, channels), bf16)
    dma = pltpu.SemaphoreType.DMA
    chunks = channels // min(512, channels)
    y, dz, grads = pl.pallas_call(
        functools.partial(main_kernel, rows, channels, groups, batch),
        out_shape=[
            jax.ShapeDtypeStruct((rows, channels), bf16),
            jax.ShapeDtypeStruct((rows, channels), bf16),
            jax.ShapeDtypeStruct((24, 128), f32),
        ],
        in_specs=[hbm] * 11,
        out_specs=[hbm, hbm, pl.BlockSpec(memory_space=pltpu.VMEM)],
        scratch_shapes=[pltpu.VMEM((16, channels), f32)] * 2
        + [pltpu.VMEM((1, channels), f32)]
        + [pltpu.VMEM(table.shape, bf16) for table in tables]
        + [half] * 4
        + [pltpu.VMEM((2 * rows, channels), bf16)] * 2
        + [big] * 6
        + [pltpu.VMEM((sub_rows, channels), f32)] * 2
        + [pltpu.VMEM((16, 8, channels), f32)] * 2
        + [pltpu.VMEM((16, channels), f32)] * 2
        + [pltpu.VMEM((rows // sub_rows, 16, channels), f32)] * 4
        + [pltpu.VMEM((16, 1, channels), f32)] * 4
        + [half] * 2
        + [pltpu.VMEM((groups, 17, 128), f32)] * 2
        + [pltpu.VMEM((groups, 16, 128), f32)] * 2
        + [pltpu.VMEM((groups, 2, 16, 128), bf16)] * 2
        + [pltpu.VMEM((17, 128), f32), pltpu.VMEM((batch, 17, 128), f32)]
        + [dma((4, chunks)), dma((7,)), dma((2,))]
        + [dma] * 8,
        compiler_params=pltpu.CompilerParams(
            collective_id=0, has_side_effects=True, vmem_limit_bytes=62 * 2**20
        ),
        name="hyena_main",
    )(q, k, v, o, residues, rates, skip_gain[None, :], *tables)
    tile = min(64, rows)
    rowed = pl.BlockSpec((tile, channels), lambda i: (i, 0))

    def whole(*shape):
        return pl.BlockSpec(shape, lambda i: (0, 0))

    wide16 = jax.ShapeDtypeStruct((rows, channels), bf16)
    gq, gk, gv, gr, gl, gs = pl.pallas_call(
        gate_kernel,
        grid=(rows // tile,),
        out_shape=[wide16] * 3
        + [jax.ShapeDtypeStruct((16, 64), f32)] * 2
        + [jax.ShapeDtypeStruct((1, 64), f32)],
        in_specs=[rowed] * 5 + [whole(24, 128)],
        out_specs=[rowed] * 3 + [whole(16, 64), whole(16, 64), whole(1, 64)],
        compiler_params=pltpu.CompilerParams(vmem_limit_bytes=62 * 2**20),
        name="hyena_gate",
    )(o, k, v, y, dz, grads)
    return gq[None], gk[None], gv[None], gr, gl, gs[0]


def solution(mesh):
    row_spec = P("dp", "seq", None)
    return jax.shard_map(
        shards,
        mesh=mesh,
        in_specs=(row_spec,) * 4 + (P(),) * 3,
        out_specs=(row_spec,) * 3 + (P(None, "seq"), P(None, "seq"), P("seq")),
        check_vma=False,
    )
```

```python
import functools

import jax
import jax.numpy as jnp
import ml_dtypes
import numpy as np
from jax import lax
from jax.experimental import pallas as pl
from jax.experimental.pallas import tpu as pltpu
from jax.sharding import PartitionSpec as P

MESH = pl.DeviceIdType.MESH
f32 = jnp.float32
bf16 = jnp.bfloat16


def split_table(table):
    high = table.astype(ml_dtypes.bfloat16)
    low = (table - high.astype(np.float64)).astype(ml_dtypes.bfloat16)
    return high, low


def dft_tables(rows):
    odd = 2 * np.arange(rows)[:, None] + 1
    angle = np.pi / (2 * rows) * (odd * np.arange(rows)[None, :] % (4 * rows))
    forward = np.concatenate([np.cos(angle), -np.sin(angle)], axis=0)
    inverse = np.concatenate([np.cos(angle).T, -np.sin(angle).T], axis=1) / rows
    return forward, inverse


def stacked_tables(rows, sub_rows):
    forward, inverse = dft_tables(rows)
    sub_fwd, sub_inv = dft_tables(sub_rows)
    parts = rows // sub_rows
    blocks = np.zeros((2, sub_rows, parts, parts, sub_rows))
    for part in range(parts):
        blocks[:, :, part, part, :] = sub_fwd.reshape(2, sub_rows, sub_rows)
    blocks = blocks.transpose(0, 2, 1, 3, 4).reshape(2 * rows, rows)
    fwd = np.concatenate(split_table(forward), axis=1)
    inv = np.concatenate(split_table(inverse), axis=0)
    fwd_sub = np.concatenate(split_table(blocks), axis=1)
    inv_sub = np.concatenate(split_table(sub_inv), axis=0)
    return fwd, inv, fwd_sub, inv_sub


def main_kernel(
    rows,
    channels,
    groups,
    batch,
    q_hbm,
    k_hbm,
    v_hbm,
    o_hbm,
    res_hbm,
    rates_hbm,
    gain_hbm,
    fwd_hbm,
    inv_hbm,
    fsub_hbm,
    isub_hbm,
    y_hbm,
    dz_hbm,
    grad_ref,
    res_ref,
    rates_ref,
    gain_ref,
    fwd_ref,
    inv_ref,
    fsub_ref,
    isub_ref,
    q_in,
    k_in,
    v_in,
    o_in,
    prod_h,
    carr_h,
    prod_f,
    carr_f,
    conv_s,
    back_s,
    lag_s,
    up_tab,
    down_tab,
    gam_one,
    gam_sub,
    sub_s,
    sub_b,
    sub_s1,
    sub_b1,
    gam_eight,
    y_out,
    dz_out,
    span_t,
    send_a,
    pair_a,
    chip_a,
    recv_a,
    send_b,
    recv_b,
    send_l,
    pair_l,
    chip_l,
    recv_l,
    send_g,
    recv_g,
    in_sem,
    small_sem,
    out_sem,
    pa_send,
    pa_recv,
    a_send,
    a_recv,
    b_send,
    b_recv,
    f_send,
    f_recv,
    pl_send,
    pl_recv,
    l_send,
    l_recv,
    g_send,
    g_recv,
):
    length = rows * groups
    inv_len = 1.0 / length
    sub_rows = isub_ref.shape[0] // 2
    parts = rows // sub_rows
    ny = min(4, groups // 2)
    nx = groups // (2 * ny)
    chunks = nx
    wide = channels // chunks
    mid = min(256, channels)
    me = lax.axis_index("seq")
    me_b = lax.axis_index("dp")

    chips = groups // 2
    my_chip = me // 2
    core = lax.rem(me, 2)
    first_core = core == 0
    sibling = me + 1 - 2 * core

    def dp_peer(step):
        return lax.rem(me_b + step, batch)

    def lanes_of(index, size):
        return pl.ds(pl.multiple_of(index * size, size), size)

    my_x = me // (2 * ny)
    my_y = lax.rem(me // 2, ny)

    def spread(index, size):
        return lax.rem(index * (index + 1) // 2, size)

    def chip_at(index):
        x = lax.rem(my_x + spread(lax.rem(index, nx), nx), nx)
        y = lax.rem(my_y + spread(index // nx, ny), ny)
        return x * ny + y

    def chunk_at(step):
        return lax.rem(my_x + (chunks - 1 - step) * (chunks - step) // 2, chunks)

    def in_copies(step):
        lanes = lanes_of(chunk_at(step), wide)
        return [
            pltpu.make_async_copy(src.at[:, lanes], dst.at[:, lanes], in_sem.at[which, step])
            for which, (src, dst) in enumerate(
                ((k_hbm, k_in), (v_hbm, v_in), (o_hbm, o_in), (q_hbm, q_in))
            )
        ]

    small = [
        pltpu.make_async_copy(src, dst, small_sem.at[which])
        for which, (src, dst) in enumerate(
            (
                (rates_hbm, rates_ref),
                (res_hbm, res_ref),
                (gain_hbm, gain_ref),
                (fwd_hbm, fwd_ref),
                (inv_hbm, inv_ref),
                (fsub_hbm, fsub_ref),
                (isub_hbm, isub_ref),
            )
        )
    ]
    for copy in small[:2]:
        copy.start()
    for step in range(chunks):
        for copy in in_copies(step):
            copy.start()
    for copy in small[2:]:
        copy.start()

    barrier = pltpu.get_barrier_semaphore()

    def greet_chip(step, _):
        peer = 2 * lax.rem(my_chip + step, chips) + core
        pl.semaphore_signal(barrier, inc=1, device_id={"seq": peer}, device_id_type=MESH)
        return 0

    def greet_dp(step, _):
        pl.semaphore_signal(barrier, inc=1, device_id={"dp": dp_peer(step)}, device_id_type=MESH)
        return 0

    lax.fori_loop(1, chips, greet_chip, 0)
    pl.semaphore_signal(barrier, inc=1, device_id={"seq": sibling}, device_id_type=MESH)
    lax.fori_loop(1, batch, greet_dp, 0)

    for copy in small[:2]:
        copy.wait()
    decay_all = rates_ref[...] * inv_len
    gam_one[...] = jnp.exp(-decay_all)
    gam_sub[...] = jnp.exp(-float(sub_rows) * decay_all)
    lane = lax.broadcasted_iota(jnp.int32, (8, 128), 1)
    left = lane < 64

    def pack(block):
        top = block[0:8]
        low = block[8:16]
        return (
            jnp.where(left, top, pltpu.roll(low, 64, 1)),
            jnp.where(left, pltpu.roll(top, 64, 1), low),
        )

    def horner(up_refs, down_refs, base, lanes, width, weighted):
        gamma = gam_one[:, lanes]
        totals = [jnp.zeros((16, width), f32)] * (len(up_refs) + len(down_refs))
        ups = len(up_refs)
        row = lax.broadcasted_iota(jnp.int32, (8, width), 0).astype(f32)
        for i in range(sub_rows // 8):
            ups_in = [ref[pl.ds(pl.multiple_of(base + i * 8, 8), 8), lanes] for ref in up_refs]
            at = sub_rows - 8 - i * 8
            low = pl.multiple_of(base + at, 8)
            downs_in = [ref[pl.ds(low, 8), lanes] for ref in down_refs]
            if weighted:
                ups_in = [block * (float(sub_rows - i * 8) - row) for block in ups_in]
                downs_in = [
                    block * (float(at) + row) if flag else block
                    for block, flag in zip(downs_in, weighted)
                ]
            for r in range(8):
                for which, block in enumerate(ups_in):
                    totals[which] = totals[which] * gamma + block[r : r + 1]
                for which, block in enumerate(downs_in):
                    totals[ups + which] = totals[ups + which] * gamma + block[7 - r : 8 - r]
        return [t * gamma for t in totals[:ups]] + totals[ups:]

    for step in range(chunks):
        chunk = chunk_at(step)
        lanes = lanes_of(chunk, wide)
        for copy in in_copies(step):
            copy.wait()
        prod = (k_in[:, lanes].astype(f32) * v_in[:, lanes].astype(f32)).astype(bf16)
        carr = (o_in[:, lanes].astype(f32) * q_in[:, lanes].astype(f32)).astype(bf16)
        prod_h[:, lanes] = prod
        carr_h[:, lanes] = carr
        prod_32 = prod.astype(f32)
        carr_32 = carr.astype(f32)
        prod_f[:, lanes] = prod_32
        carr_f[:, lanes] = carr_32
        skip = jnp.sum(prod_32 * carr_32, axis=0, keepdims=True)

        def state_body(part, _):
            base = pl.multiple_of(part * sub_rows, sub_rows)
            sub_s[part, :, lanes], sub_b[part, :, lanes] = horner(
                [prod_f], [carr_f], base, lanes, wide, None
            )
            return 0

        lax.fori_loop(0, parts, state_body, 0)
        ratio = gam_sub[:, lanes]
        state_p = sub_s[0, :, lanes]
        state_c = sub_b[parts - 1, :, lanes]
        for part in range(1, parts):
            state_p = state_p * ratio + sub_s[part, :, lanes]
            state_c = state_c * ratio + sub_b[parts - 1 - part, :, lanes]
        for part in range(wide // 128):
            cut = slice(part * 128, part * 128 + 128)
            pair = chunk * (wide // 128) + part
            for half, (p_tile, c_tile) in enumerate(zip(pack(state_p[:, cut]), pack(state_c[:, cut]))):
                send_a[half, pair, 0:8, :] = p_tile
                send_a[half, pair, 8:16, :] = c_tile
            row = skip[:, cut]
            send_a[0, pair, 16:17, :] = row
            send_a[1, pair, 16:17, :] = pltpu.roll(row, 64, 1)

    pl.semaphore_wait(barrier, chips + batch - 1)

    def pair_copy(src, dst, send_sem, recv_sem):
        return pltpu.make_async_remote_copy(
            src_ref=src,
            dst_ref=dst,
            send_sem=send_sem,
            recv_sem=recv_sem,
            device_id={"seq": sibling},
            device_id_type=MESH,
        )

    pair_copy(send_a, pair_a, pa_send, pa_recv).start()

    def span_body(j, _):
        lanes = lanes_of(j, 128)
        span = jnp.exp(rates_ref[:, lanes] * (-inv_len * float(rows)))
        span_t[0, j], span_t[1, j] = pack(span)
        return 0

    lax.fori_loop(0, chips, span_body, 0, unroll=4)
    pltpu.make_async_copy(pair_a, pair_a, pa_recv).wait()

    def ordered(own, other):
        return jnp.where(first_core, own, other), jnp.where(first_core, other, own)

    def to_chip(src, dst, peer_chip, send_sem, recv_sem):
        return pltpu.make_async_remote_copy(
            src_ref=src.at[peer_chip],
            dst_ref=dst.at[my_chip],
            send_sem=send_sem,
            recv_sem=recv_sem,
            device_id={"seq": 2 * peer_chip + core},
            device_id_type=MESH,
        )

    def chip_states(i, _):
        j = chip_at(chips - 1 - i)
        span = span_t[core, j]
        p_first, p_second = ordered(send_a[core, j, 0:8, :], pair_a[core, j, 0:8, :])
        c_first, c_second = ordered(send_a[core, j, 8:16, :], pair_a[core, j, 8:16, :])
        chip_a[j, 0:8, :] = span * p_first + p_second
        chip_a[j, 8:16, :] = c_first + span * c_second
        chip_a[j, 16:17, :] = send_a[core, j, 16:17, :] + pair_a[core, j, 16:17, :]

        @pl.when(j != my_chip)
        def _():
            to_chip(chip_a, recv_a, j, a_send, a_recv).start()

        return 0

    lax.fori_loop(0, chips, chip_states, 0)
    recv_a[my_chip] = chip_a[my_chip]


    def synth(coefs, table, lanes, ascending):
        count = rows // 8
        waves = [table[n, :, lanes] * coefs[n // 8][n % 8 : n % 8 + 1] for n in range(16)]
        ratios = [jnp.broadcast_to(gam_eight[n, :, lanes], (8, 128)) for n in range(16)]
        blocks = []
        for order in range(count):
            terms = waves
            while len(terms) > 1:
                terms = [terms[i] + terms[i + 1] for i in range(0, len(terms), 2)]
            blocks.append(terms[0])
            if order < count - 1:
                waves = [wave * ratio for wave, ratio in zip(waves, ratios)]
        return jnp.concatenate(blocks if ascending else blocks[::-1], axis=0)

    def dot(a, b):
        return jnp.dot(a, b, preferred_element_type=f32)

    for copy in small[2:]:
        copy.wait()

    def lag_body(j, _):
        lanes = lanes_of(j, mid)
        table = fsub_ref[...]
        prod = prod_h[:, lanes]
        carr = carr_h[:, lanes]
        spec_p = dot(table, jnp.concatenate([prod, prod], axis=0))
        spec_c = dot(table, jnp.concatenate([carr, carr], axis=0))
        real = jnp.zeros((sub_rows, mid), f32)
        imag = jnp.zeros((sub_rows, mid), f32)
        for part in range(parts):
            lo = part * sub_rows
            pr, pi = spec_p[lo : lo + sub_rows], spec_p[rows + lo : rows + lo + sub_rows]
            cr, ci = spec_c[lo : lo + sub_rows], spec_c[rows + lo : rows + lo + sub_rows]
            real = real + (cr * pr + ci * pi)
            imag = imag + (ci * pr - cr * pi)
        both = dot(isub_ref[...], jnp.concatenate([real.astype(bf16), imag.astype(bf16)], axis=0))
        lag_s[:, lanes] = both[:sub_rows] + both[sub_rows:]
        return 0

    lax.fori_loop(0, channels // mid, lag_body, 0)

    def moments_body(j, _):
        lanes = lanes_of(j, wide)

        def slope_body(part, _):
            base = pl.multiple_of(part * sub_rows, sub_rows)
            sub_s1[part, :, lanes], sub_b1[part, :, lanes] = horner(
                [prod_f], [carr_f], base, lanes, wide, (True,)
            )
            return 0

        lax.fori_loop(0, parts, slope_body, 0)
        lag_0, lag_1 = horner([], [lag_s, lag_s], 0, lanes, wide, (False, True))
        for part in range(wide // 128):
            cut = slice(part * 128, part * 128 + 128)
            pair = j * (wide // 128) + part
            own = lanes_of(pair, 128)
            ratio = gam_sub[:, own]
            total_0, total_1 = lag_0[:, cut], lag_1[:, cut]
            state, slope = sub_s[0, :, own], sub_s1[0, :, own]
            for q in range(1, parts):
                c_state = sub_b[q, :, own]
                total_0 = total_0 + c_state * state
                total_1 = total_1 + sub_b1[q, :, own] * state + c_state * slope
                slope = ratio * (slope + float(sub_rows) * state) + sub_s1[q, :, own]
                state = ratio * state + sub_s[q, :, own]
            c_slope = sub_b1[parts - 1, :, own]
            c_state = sub_b[parts - 1, :, own]
            for q in range(parts - 2, -1, -1):
                c_slope = ratio * (c_slope + float(sub_rows) * c_state) + sub_b1[q, :, own]
                c_state = ratio * c_state + sub_b[q, :, own]
            tiles = [pack(x) for x in (slope, c_slope, total_0, total_1)]
            for half in range(2):
                send_l[half, pair, 0] = jnp.concatenate(
                    [tiles[0][half], tiles[1][half]], axis=0
                ).astype(bf16)
                send_l[half, pair, 1] = jnp.concatenate(
                    [tiles[2][half], tiles[3][half]], axis=0
                ).astype(bf16)
        return 0

    lax.fori_loop(0, channels // wide, moments_body, 0)

    pair_copy(send_l.at[1 - core], pair_l, pl_send, pl_recv).start()

    def table_body(n, _):
        rate = rates_ref[pl.ds(n, 1), :] * inv_len
        sub = lax.broadcasted_iota(jnp.int32, (8, channels), 0).astype(f32)
        gam_eight[n] = jnp.exp(-8.0 * rate)
        up_tab[n] = jnp.exp(-rate * sub)
        down_tab[n] = jnp.exp(-rate * (8.0 - sub))
        return 0

    lax.fori_loop(0, 16, table_body, 0)

    pltpu.make_async_copy(pair_l, pair_l, pl_recv).wait()

    def chip_sums(i, _):
        j = chip_at(chips - 1 - i)
        span = span_t[core, j]
        p_first, _ = ordered(send_a[core, j, 0:8, :], pair_a[core, j, 0:8, :])
        _, c_second = ordered(send_a[core, j, 8:16, :], pair_a[core, j, 8:16, :])
        own_slope, own_lag = send_l[core, j, 0].astype(f32), send_l[core, j, 1].astype(f32)
        pair_slope, pair_lag = pair_l[j, 0].astype(f32), pair_l[j, 1].astype(f32)
        sp_first, sp_second = ordered(own_slope[0:8], pair_slope[0:8])
        sc_first, sc_second = ordered(own_slope[8:16], pair_slope[8:16])
        lags = own_lag + pair_lag
        chip_l[j, 0] = jnp.concatenate(
            [
                span * (sp_first + float(rows) * p_first) + sp_second,
                sc_first + span * (sc_second + float(rows) * c_second),
            ],
            axis=0,
        ).astype(bf16)
        chip_l[j, 1] = jnp.concatenate(
            [
                lags[0:8] + c_second * p_first,
                lags[8:16] + (sc_second * p_first + c_second * sp_first),
            ],
            axis=0,
        ).astype(bf16)

        @pl.when(j != my_chip)
        def _():
            to_chip(chip_l, recv_l, j, l_send, l_recv).start()

        return 0

    lax.fori_loop(0, chips, chip_sums, 0)
    recv_l[my_chip] = chip_l[my_chip]

    def conv_body(j, _):
        lanes = lanes_of(j, mid)
        taps = jnp.concatenate(
            [
                synth((res_ref[0:8, own], res_ref[8:16, own]), up_tab, own, True)
                for own in [lanes_of(j * (mid // 128) + part, 128) for part in range(mid // 128)]
            ],
            axis=1,
        )
        high = taps.astype(bf16)
        low = (taps - high.astype(f32)).astype(bf16)
        table = fwd_ref[...]
        filt = dot(table, jnp.concatenate([high, high], axis=0)) + dot(table[:, :rows], low)
        prod = prod_h[:, lanes]
        carr = carr_h[:, lanes]
        spec_p = dot(table, jnp.concatenate([prod, prod], axis=0))
        spec_c = dot(table, jnp.concatenate([carr, carr], axis=0))
        fr, fi = filt[:rows], filt[rows:]
        pr, pi = spec_p[:rows], spec_p[rows:]
        cr, ci = spec_c[:rows], spec_c[rows:]
        inverse = inv_ref[...]

        def back_to_rows(real, imag):
            spec = jnp.concatenate([real.astype(bf16), imag.astype(bf16)], axis=0)
            both = dot(inverse, spec)
            return both[:rows] + both[rows:]

        conv_s[:, lanes] = back_to_rows(pr * fr - pi * fi, pr * fi + pi * fr)
        back_s[:, lanes] = back_to_rows(cr * fr + ci * fi, ci * fr - cr * fi)
        return 0

    conv_steps = channels // mid
    conv_early = conv_steps // 2
    lax.fori_loop(0, conv_early, conv_body, 0)

    def wait_bytes(ref, sem, count):
        block = ref.at[pl.ds(0, count)]
        pltpu.make_async_copy(block, block, sem).wait()

    wait_bytes(recv_a, a_recv, chips - 1)
    own_lanes = lanes_of(my_chip, 128)

    def own_pack(block):
        first, second = pack(block)
        return jnp.where(first_core, first, second)

    own_decay = own_pack(rates_ref[:, own_lanes]) * inv_len
    own_res = own_pack(res_ref[:, own_lanes])
    span = jnp.exp(-own_decay * float(2 * rows))
    zero = jnp.zeros((8, 128), f32)

    def up_scan(i, carry):
        state, slope, total, moment = carry
        p_in = recv_a[i, 0:8, :]
        c_in = recv_a[i, 8:16, :]
        send_b[i, 0:8, :] = state
        total = total + c_in * state
        moment = moment + c_in * slope
        slope = span * (slope + state)
        state = span * state + p_in
        return state, slope, total, moment

    _, _, total, moment = lax.fori_loop(0, chips, up_scan, (zero, zero, zero, zero), unroll=4)

    def down_scan(i, state):
        at = chips - 1 - i
        send_b[at, 8:16, :] = state
        return span * state + recv_a[at, 8:16, :]

    lax.fori_loop(0, chips, down_scan, zero, unroll=4)

    def send_b_body(i, _):
        j = chip_at(chips - 1 - i)

        @pl.when(j != my_chip)
        def _():
            pltpu.make_async_remote_copy(
                src_ref=send_b.at[j],
                dst_ref=recv_b.at[core, my_chip],
                send_sem=b_send,
                recv_sem=b_recv.at[my_chip],
                device_id={"seq": 2 * j + core},
                device_id_type=MESH,
            ).start()

        return 0

    lax.fori_loop(0, chips, send_b_body, 0)
    recv_b[core, my_chip] = send_b[my_chip]

    def skip_body(i, acc):
        return acc + recv_a[i, 16:17, :]

    skip_sum = lax.fori_loop(0, chips, skip_body, jnp.zeros((1, 128), f32))

    lax.fori_loop(conv_early, conv_steps, conv_body, 0)

    wait_bytes(recv_l, l_recv, chips - 1)

    def combine_body(i, carry):
        grad_0, grad_1 = carry
        slopes = recv_l[i, 0].astype(f32)
        lags = recv_l[i, 1].astype(f32)
        grad_0 = grad_0 + lags[0:8]
        grad_1 = grad_1 + lags[8:16]
        grad_1 = grad_1 + slopes[8:16] * send_b[i, 0:8, :] + slopes[0:8] * send_b[i, 8:16, :]
        return grad_0, grad_1

    grad_0, grad_1 = lax.fori_loop(
        0, chips, combine_body, (total, float(2 * rows) * moment), unroll=4
    )
    send_g[0:8, :] = grad_0 * inv_len
    send_g[8:16, :] = -own_res * own_decay * grad_1 * inv_len
    send_g[16:17, :] = skip_sum * inv_len

    def send_g_body(step, _):
        pltpu.make_async_remote_copy(
            src_ref=send_g,
            dst_ref=recv_g.at[me_b],
            send_sem=g_send,
            recv_sem=g_recv,
            device_id={"dp": dp_peer(step)},
            device_id_type=MESH,
        ).start()
        return 0

    lax.fori_loop(1, batch, send_g_body, 0)
    recv_g[me_b] = send_g[...]
    def out_copies(j):
        lanes = lanes_of(j, 128)
        return [
            pltpu.make_async_copy(src.at[:, lanes], dst.at[:, lanes], out_sem.at[which])
            for which, (src, dst) in enumerate(((y_out, y_hbm), (dz_out, dz_hbm)))
        ]

    def forward(i):
        j = chip_at(i)
        block = recv_b.at[core, j]

        @pl.when(j != my_chip)
        def _():
            pltpu.make_async_copy(block, block, b_recv.at[j]).wait()

        pair_copy(block, block, f_send, f_recv.at[j]).start()

    ahead = min(3, chips)
    for i in range(ahead):
        forward(i)

    def final_body(i, _):
        @pl.when(i + ahead < chips)
        def _():
            forward(i + ahead)

        j = chip_at(i)
        other = recv_b.at[1 - core, j]
        pltpu.make_async_copy(other, other, f_recv.at[j]).wait()
        lanes = lanes_of(j, 128)
        res = res_ref[:, lanes]
        far = []
        for half, far_core, table, ascending in ((0, 1, up_tab, True), (8, 0, down_tab, False)):
            states = []
            for part in range(2):
                state = recv_b[part, j, half : half + 8, :]
                farther = span_t[part, j] * state + pair_a[part, j, half : half + 8, :]
                states.append(jnp.where(core == far_core, farther, state))
            first, second = states
            low = res[0:8] * jnp.where(left, first, pltpu.roll(second, 64, 1))
            high = res[8:16] * jnp.where(left, pltpu.roll(first, 64, 1), second)
            far.append(synth((low, high), table, lanes, ascending))
        conv = conv_s[:, lanes] + far[0]
        back = back_s[:, lanes] + far[1]
        gain = gain_ref[:, lanes]
        y_out[:, lanes] = (conv.astype(bf16).astype(f32) + gain * prod_f[:, lanes]).astype(bf16)
        dz_out[:, lanes] = (back.astype(bf16).astype(f32) + gain * carr_f[:, lanes]).astype(bf16)
        for copy in out_copies(j):
            copy.start()
        return 0

    lax.fori_loop(0, chips, final_body, 0)

    wait_bytes(recv_g, g_recv, batch - 1)

    def total_body(i, acc):
        return acc + recv_g[i]

    grad_ref[0:17, :] = lax.fori_loop(0, batch, total_body, jnp.zeros((17, 128), f32))

    pltpu.make_async_copy(send_a, send_a, pa_send).wait()
    pltpu.make_async_copy(pair_l, pair_l, pl_send).wait()
    wait_bytes(chip_a, a_send, chips - 1)
    wait_bytes(send_b, b_send, chips - 1)
    wait_bytes(chip_l, l_send, chips - 1)
    wait_bytes(send_b, f_send, chips)
    wait_bytes(recv_g, g_send, batch - 1)

    def drain(j, _):
        for copy in out_copies(j):
            copy.wait()
        return 0

    lax.fori_loop(0, chips, drain, 0)


def gate_kernel(cot, key, value, y, dz, grads, grad_q, grad_k, grad_v, grad_r, grad_l, grad_s):
    dz_now = dz[...].astype(f32)
    grad_q[...] = (cot[...].astype(f32) * y[...].astype(f32)).astype(bf16)
    grad_k[...] = (dz_now * value[...].astype(f32)).astype(bf16)
    grad_v[...] = (dz_now * key[...].astype(f32)).astype(bf16)

    @pl.when(pl.program_id(0) == 0)
    def _():
        for start, out in ((0, grad_r), (8, grad_l)):
            tile = grads[start : start + 8, :]
            out[0:8, :] = tile[:, 0:64]
            out[8:16, :] = pltpu.roll(tile, 64, 1)[:, 0:64]
        grad_s[...] = grads[16:17, 0:64]


def shards(queries, key_branch, value_branch, cotangent, residues, rates, skip_gain):
    groups = lax.axis_size("seq")
    batch = lax.axis_size("dp")
    rows, channels = queries.shape[1:]
    sub_rows = 32
    tables = [jnp.asarray(table) for table in stacked_tables(rows, sub_rows)]
    q, k, v, o = (x[0] for x in (queries, key_branch, value_branch, cotangent))
    hbm = pl.BlockSpec(memory_space=pltpu.HBM)
    big = pltpu.VMEM((rows, channels), f32)
    half = pltpu.VMEM((rows, channels), bf16)
    dma = pltpu.SemaphoreType.DMA
    chips = groups // 2
    chunks = chips // min(4, chips)
    y, dz, grads = pl.pallas_call(
        functools.partial(main_kernel, rows, channels, groups, batch),
        out_shape=[
            jax.ShapeDtypeStruct((rows, channels), bf16),
            jax.ShapeDtypeStruct((rows, channels), bf16),
            jax.ShapeDtypeStruct((24, 128), f32),
        ],
        in_specs=[hbm] * 11,
        out_specs=[hbm, hbm, pl.BlockSpec(memory_space=pltpu.VMEM)],
        scratch_shapes=[pltpu.VMEM((16, channels), f32)] * 2
        + [pltpu.VMEM((1, channels), f32)]
        + [pltpu.VMEM(table.shape, bf16) for table in tables]
        + [half] * 6
        + [big] * 4
        + [pltpu.VMEM((sub_rows, channels), f32)]
        + [pltpu.VMEM((16, 8, channels), f32)] * 2
        + [pltpu.VMEM((16, channels), f32)] * 2
        + [pltpu.VMEM((rows // sub_rows, 16, channels), f32)] * 4
        + [pltpu.VMEM((16, 1, channels), f32)]
        + [half] * 2
        + [pltpu.VMEM((2, chips, 8, 128), f32)]
        + [pltpu.VMEM((2, chips, 17, 128), f32)] * 2
        + [pltpu.VMEM((chips, 17, 128), f32)] * 2
        + [pltpu.VMEM((chips, 16, 128), f32)]
        + [pltpu.VMEM((2, chips, 16, 128), f32)]
        + [pltpu.VMEM((2, chips, 2, 16, 128), bf16)]
        + [pltpu.VMEM((chips, 2, 16, 128), bf16)] * 3
        + [pltpu.VMEM((17, 128), f32), pltpu.VMEM((batch, 17, 128), f32)]
        + [dma((4, chunks)), dma((7,)), dma((2,))]
        + [dma] * 5
        + [dma((chips,)), dma, dma((chips,))]
        + [dma] * 6,
        compiler_params=pltpu.CompilerParams(
            collective_id=0, has_side_effects=True, vmem_limit_bytes=62 * 2**20
        ),
        name="hyena_main",
    )(q, k, v, o, residues, rates, skip_gain[None, :], *tables)
    tile = min(64, rows)
    rowed = pl.BlockSpec((tile, channels), lambda i: (i, 0))

    def whole(*shape):
        return pl.BlockSpec(shape, lambda i: (0, 0))

    wide16 = jax.ShapeDtypeStruct((rows, channels), bf16)
    gq, gk, gv, gr, gl, gs = pl.pallas_call(
        gate_kernel,
        grid=(rows // tile,),
        out_shape=[wide16] * 3
        + [jax.ShapeDtypeStruct((16, 64), f32)] * 2
        + [jax.ShapeDtypeStruct((1, 64), f32)],
        in_specs=[rowed] * 5 + [whole(24, 128)],
        out_specs=[rowed] * 3 + [whole(16, 64), whole(16, 64), whole(1, 64)],
        compiler_params=pltpu.CompilerParams(vmem_limit_bytes=62 * 2**20),
        name="hyena_gate",
    )(o, k, v, y, dz, grads)
    return gq[None], gk[None], gv[None], gr, gl, gs[0]


def solution(mesh):
    row_spec = P("dp", "seq", None)
    return jax.shard_map(
        shards,
        mesh=mesh,
        in_specs=(row_spec,) * 4 + (P(),) * 3,
        out_specs=(row_spec,) * 3 + (P(None, "seq"), P(None, "seq"), P("seq")),
        check_vma=False,
    )
```

```python
import functools

import jax
import jax.numpy as jnp
import ml_dtypes
import numpy as np
from jax import lax
from jax.experimental import pallas as pl
from jax.experimental.pallas import tpu as pltpu
from jax.sharding import PartitionSpec as P

MESH = pl.DeviceIdType.MESH
f32 = jnp.float32
bf16 = jnp.bfloat16


def split_table(table):
    high = table.astype(ml_dtypes.bfloat16)
    low = (table - high.astype(np.float64)).astype(ml_dtypes.bfloat16)
    return high, low


def dft_tables(rows):
    odd = 2 * np.arange(rows)[:, None] + 1
    angle = np.pi / (2 * rows) * (odd * np.arange(rows)[None, :] % (4 * rows))
    forward = np.concatenate([np.cos(angle), -np.sin(angle)], axis=0)
    inverse = np.concatenate([np.cos(angle).T, -np.sin(angle).T], axis=1) / rows
    return forward, inverse


def stacked_tables(rows, sub_rows):
    forward, inverse = dft_tables(rows)
    sub_fwd, sub_inv = dft_tables(sub_rows)
    parts = rows // sub_rows
    blocks = np.zeros((2, sub_rows, parts, parts, sub_rows))
    for part in range(parts):
        blocks[:, :, part, part, :] = sub_fwd.reshape(2, sub_rows, sub_rows)
    blocks = blocks.transpose(0, 2, 1, 3, 4).reshape(2 * rows, rows)
    fwd = np.concatenate(split_table(forward), axis=1)
    inv = np.concatenate(split_table(inverse), axis=0)
    fwd_sub = np.concatenate(split_table(blocks), axis=1)
    inv_sub = np.concatenate(split_table(sub_inv), axis=0)
    return fwd, inv, fwd_sub, inv_sub


def main_kernel(
    rows,
    channels,
    groups,
    batch,
    q_hbm,
    k_hbm,
    v_hbm,
    o_hbm,
    res_hbm,
    rates_hbm,
    gain_hbm,
    fwd_hbm,
    inv_hbm,
    fsub_hbm,
    isub_hbm,
    y_hbm,
    dz_hbm,
    grad_ref,
    res_ref,
    rates_ref,
    gain_ref,
    fwd_ref,
    inv_ref,
    fsub_ref,
    isub_ref,
    q_in,
    k_in,
    v_in,
    o_in,
    prod_h,
    carr_h,
    prod_f,
    carr_f,
    conv_s,
    back_s,
    lag_s,
    up_tab,
    down_tab,
    gam_one,
    gam_sub,
    sub_s,
    sub_b,
    sub_s1,
    sub_b1,
    lag_0,
    lag_1,
    gam_eight,
    y_out,
    dz_out,
    span_t,
    send_a,
    pair_a,
    chip_a,
    recv_a,
    send_b,
    recv_b,
    send_l,
    pair_l,
    chip_l,
    recv_l,
    send_g,
    recv_g,
    in_sem,
    small_sem,
    out_sem,
    pa_send,
    pa_recv,
    a_send,
    a_recv,
    b_send,
    b_recv,
    f_send,
    f_recv,
    pl_send,
    pl_recv,
    l_send,
    l_recv,
    g_send,
    g_recv,
):
    length = rows * groups
    inv_len = 1.0 / length
    sub_rows = isub_ref.shape[0] // 2
    parts = rows // sub_rows
    ny = min(4, groups // 2)
    nx = groups // (2 * ny)
    chunks = nx
    wide = channels // chunks
    mid = min(512, channels)
    me = lax.axis_index("seq")
    me_b = lax.axis_index("dp")

    chips = groups // 2
    my_chip = me // 2
    core = lax.rem(me, 2)
    first_core = core == 0
    sibling = me + 1 - 2 * core

    def dp_peer(step):
        return lax.rem(me_b + step, batch)

    def lanes_of(index, size):
        return pl.ds(pl.multiple_of(index * size, size), size)

    my_x = me // (2 * ny)
    my_y = lax.rem(me // 2, ny)

    def spread(index, size):
        return lax.rem(index * (index + 1) // 2, size)

    def chip_at(index):
        x = lax.rem(my_x + spread(lax.rem(index, nx), nx), nx)
        y = lax.rem(my_y + spread(index // nx, ny), ny)
        return x * ny + y

    def chunk_at(step):
        return lax.rem(my_x + (chunks - 1 - step) * (chunks - step) // 2, chunks)

    def in_copies(step):
        lanes = lanes_of(chunk_at(step), wide)
        return [
            pltpu.make_async_copy(src.at[:, lanes], dst.at[:, lanes], in_sem.at[which, step])
            for which, (src, dst) in enumerate(
                ((k_hbm, k_in), (v_hbm, v_in), (o_hbm, o_in), (q_hbm, q_in))
            )
        ]

    small = [
        pltpu.make_async_copy(src, dst, small_sem.at[which])
        for which, (src, dst) in enumerate(
            (
                (rates_hbm, rates_ref),
                (res_hbm, res_ref),
                (gain_hbm, gain_ref),
                (fwd_hbm, fwd_ref),
                (inv_hbm, inv_ref),
                (fsub_hbm, fsub_ref),
                (isub_hbm, isub_ref),
            )
        )
    ]
    for copy in small[:2]:
        copy.start()
    for step in range(chunks):
        for copy in in_copies(step):
            copy.start()
    for copy in small[2:]:
        copy.start()

    barrier = pltpu.get_barrier_semaphore()

    def greet_chip(step, _):
        peer = 2 * lax.rem(my_chip + step, chips) + core
        pl.semaphore_signal(barrier, inc=1, device_id={"seq": peer}, device_id_type=MESH)
        return 0

    def greet_dp(step, _):
        pl.semaphore_signal(barrier, inc=1, device_id={"dp": dp_peer(step)}, device_id_type=MESH)
        return 0

    lax.fori_loop(1, chips, greet_chip, 0)
    pl.semaphore_signal(barrier, inc=1, device_id={"seq": sibling}, device_id_type=MESH)
    lax.fori_loop(1, batch, greet_dp, 0)

    for copy in small[:2]:
        copy.wait()
    decay_all = rates_ref[...] * inv_len
    gam_one[...] = jnp.exp(-decay_all)
    gam_sub[...] = jnp.exp(-float(sub_rows) * decay_all)
    lane = lax.broadcasted_iota(jnp.int32, (8, 128), 1)
    left = lane < 64

    def pack(block):
        top = block[0:8]
        low = block[8:16]
        return (
            jnp.where(left, top, pltpu.roll(low, 64, 1)),
            jnp.where(left, pltpu.roll(top, 64, 1), low),
        )

    def horner(jobs, lanes, width):
        gamma = gam_one[:, lanes]
        totals = [jnp.zeros((16, width), f32)] * len(jobs)
        row = lax.broadcasted_iota(jnp.int32, (8, width), 0).astype(f32)
        for i in range(sub_rows // 8):
            at = sub_rows - 8 - i * 8
            blocks = []
            for ref, base, up, weighted in jobs:
                start = pl.multiple_of(base + (i * 8 if up else at), 8)
                block = ref[pl.ds(start, 8), lanes]
                if weighted:
                    block = block * (float(sub_rows - i * 8) - row if up else float(at) + row)
                blocks.append(block)
            for r in range(8):
                for which, (job, block) in enumerate(zip(jobs, blocks)):
                    x = block[r : r + 1] if job[2] else block[7 - r : 8 - r]
                    totals[which] = totals[which] * gamma + x
        return [t * gamma if job[2] else t for t, job in zip(totals, jobs)]

    for step in range(chunks):
        chunk = chunk_at(step)
        lanes = lanes_of(chunk, wide)
        for copy in in_copies(step):
            copy.wait()
        prod = (k_in[:, lanes].astype(f32) * v_in[:, lanes].astype(f32)).astype(bf16)
        carr = (o_in[:, lanes].astype(f32) * q_in[:, lanes].astype(f32)).astype(bf16)
        prod_h[:, lanes] = prod
        carr_h[:, lanes] = carr
        prod_32 = prod.astype(f32)
        carr_32 = carr.astype(f32)
        prod_f[:, lanes] = prod_32
        carr_f[:, lanes] = carr_32
        skip = jnp.sum(prod_32 * carr_32, axis=0, keepdims=True)

        def state_body(part, _):
            base = pl.multiple_of(part * sub_rows, sub_rows)
            sub_s[part, :, lanes], sub_b[part, :, lanes] = horner(
                [(prod_f, base, True, False), (carr_f, base, False, False)], lanes, wide
            )
            return 0

        lax.fori_loop(0, parts, state_body, 0)
        ratio = gam_sub[:, lanes]
        state_p = sub_s[0, :, lanes]
        state_c = sub_b[parts - 1, :, lanes]
        for part in range(1, parts):
            state_p = state_p * ratio + sub_s[part, :, lanes]
            state_c = state_c * ratio + sub_b[parts - 1 - part, :, lanes]
        for part in range(wide // 128):
            cut = slice(part * 128, part * 128 + 128)
            pair = chunk * (wide // 128) + part
            for half, (p_tile, c_tile) in enumerate(zip(pack(state_p[:, cut]), pack(state_c[:, cut]))):
                send_a[half, pair, 0:8, :] = p_tile
                send_a[half, pair, 8:16, :] = c_tile
            row = skip[:, cut]
            send_a[0, pair, 16:17, :] = row
            send_a[1, pair, 16:17, :] = pltpu.roll(row, 64, 1)

    pl.semaphore_wait(barrier, chips + batch - 1)

    def pair_copy(src, dst, send_sem, recv_sem):
        return pltpu.make_async_remote_copy(
            src_ref=src,
            dst_ref=dst,
            send_sem=send_sem,
            recv_sem=recv_sem,
            device_id={"seq": sibling},
            device_id_type=MESH,
        )

    pair_copy(send_a, pair_a, pa_send, pa_recv).start()

    def span_body(j, _):
        lanes = lanes_of(j, 128)
        span = jnp.exp(rates_ref[:, lanes] * (-inv_len * float(rows)))
        span_t[0, j], span_t[1, j] = pack(span)
        return 0

    lax.fori_loop(0, chips, span_body, 0, unroll=4)
    pltpu.make_async_copy(pair_a, pair_a, pa_recv).wait()

    def ordered(own, other):
        return jnp.where(first_core, own, other), jnp.where(first_core, other, own)

    def to_chip(src, dst, peer_chip, send_sem, recv_sem):
        return pltpu.make_async_remote_copy(
            src_ref=src.at[peer_chip],
            dst_ref=dst.at[my_chip],
            send_sem=send_sem,
            recv_sem=recv_sem,
            device_id={"seq": 2 * peer_chip + core},
            device_id_type=MESH,
        )

    group = min(4, chips)

    def by_groups(compute, store, send):
        def body(i, _):
            at = [chip_at(chips - 1 - (group * i + part)) for part in range(group)]
            results = [compute(j) for j in at]
            for j, result in zip(at, results):
                store(j, result)
            for j in at:
                pl.when(j != my_chip)(functools.partial(send, j))
            return 0

        lax.fori_loop(0, chips // group, body, 0)

    def chip_states(j):
        span = span_t[core, j]
        own, other = send_a[core, j], pair_a[core, j]
        p_first, p_second = ordered(own[0:8], other[0:8])
        c_first, c_second = ordered(own[8:16], other[8:16])
        return span * p_first + p_second, c_first + span * c_second, own[16:17] + other[16:17]

    def store_states(j, result):
        chip_a[j, 0:8, :], chip_a[j, 8:16, :], chip_a[j, 16:17, :] = result

    def send_states(j):
        to_chip(chip_a, recv_a, j, a_send, a_recv).start()

    by_groups(chip_states, store_states, send_states)
    recv_a[my_chip] = chip_a[my_chip]


    def synth(coefs, table, lanes, ascending):
        count = rows // 8
        waves = [table[n, :, lanes] * coefs[n // 8][n % 8 : n % 8 + 1] for n in range(16)]
        ratios = [jnp.broadcast_to(gam_eight[n, :, lanes], (8, 128)) for n in range(16)]
        blocks = []
        for order in range(count):
            terms = waves
            while len(terms) > 1:
                terms = [terms[i] + terms[i + 1] for i in range(0, len(terms), 2)]
            blocks.append(terms[0])
            if order < count - 1:
                waves = [wave * ratio for wave, ratio in zip(waves, ratios)]
        return jnp.concatenate(blocks if ascending else blocks[::-1], axis=0)

    def dot(a, b):
        return jnp.dot(a, b, preferred_element_type=f32)

    for copy in small[2:]:
        copy.wait()

    def lag_sums(j):
        lanes = lanes_of(j, mid)
        jobs = [(lag_s, 0, False, False), (lag_s, 0, False, True)]
        lag_0[:, lanes], lag_1[:, lanes] = horner(jobs, lanes, mid)

    def lag_body(j, _):
        lanes = lanes_of(j, mid)
        table = fsub_ref[...]
        prod = prod_h[:, lanes]
        carr = carr_h[:, lanes]
        spec_p = dot(table, jnp.concatenate([prod, prod], axis=0))
        spec_c = dot(table, jnp.concatenate([carr, carr], axis=0))
        real = jnp.zeros((sub_rows, mid), f32)
        imag = jnp.zeros((sub_rows, mid), f32)
        for part in range(parts):
            lo = part * sub_rows
            pr, pi = spec_p[lo : lo + sub_rows], spec_p[rows + lo : rows + lo + sub_rows]
            cr, ci = spec_c[lo : lo + sub_rows], spec_c[rows + lo : rows + lo + sub_rows]
            real = real + (cr * pr + ci * pi)
            imag = imag + (ci * pr - cr * pi)
        both = dot(isub_ref[...], jnp.concatenate([real.astype(bf16), imag.astype(bf16)], axis=0))
        lag_s[:, lanes] = both[:sub_rows] + both[sub_rows:]
        for part in range(0, parts, 2):
            jobs = []
            for now in (part, part + 1):
                jobs.append((prod_f, now * sub_rows, True, True))
                jobs.append((carr_f, now * sub_rows, False, True))
            slopes = horner(jobs, lanes, mid)
            for now in range(2):
                sub_s1[part + now, :, lanes] = slopes[2 * now]
                sub_b1[part + now, :, lanes] = slopes[2 * now + 1]
        lag_sums(jnp.maximum(j - 1, 0))
        return 0

    lag_s[:, 0:mid] = jnp.zeros((sub_rows, mid), f32)
    lax.fori_loop(0, channels // mid, lag_body, 0)
    lag_sums(channels // mid - 1)

    def moments_of(pair):
        own = lanes_of(pair, 128)
        ratio = gam_sub[:, own]
        total_0, total_1 = lag_0[:, own], lag_1[:, own]
        p_state = [sub_s[q, :, own] for q in range(parts)]
        p_slope = [sub_s1[q, :, own] for q in range(parts)]
        c_states = [sub_b[q, :, own] for q in range(parts)]
        c_slopes = [sub_b1[q, :, own] for q in range(parts)]
        state, slope = p_state[0], p_slope[0]
        for q in range(1, parts):
            total_0 = total_0 + c_states[q] * state
            total_1 = total_1 + (c_slopes[q] * state + c_states[q] * slope)
            slope = ratio * (slope + float(sub_rows) * state) + p_slope[q]
            state = ratio * state + p_state[q]
        c_slope, c_state = c_slopes[-1], c_states[-1]
        for q in range(parts - 2, -1, -1):
            c_slope = ratio * (c_slope + float(sub_rows) * c_state) + c_slopes[q]
            c_state = ratio * c_state + c_states[q]
        tiles = [pack(x) for x in (slope, c_slope, total_0, total_1)]
        return [
            jnp.concatenate([tiles[2 * which][half], tiles[2 * which + 1][half]], axis=0).astype(bf16)
            for half in range(2)
            for which in range(2)
        ]

    def moments_body(i, _):
        pairs = [group * i + part for part in range(group)]
        results = [moments_of(pair) for pair in pairs]
        for pair, result in zip(pairs, results):
            for half in range(2):
                for which in range(2):
                    send_l[half, pair, which] = result[2 * half + which]
        return 0

    lax.fori_loop(0, chips // group, moments_body, 0)

    pair_copy(send_l.at[1 - core], pair_l, pl_send, pl_recv).start()

    def table_body(n, _):
        rate = rates_ref[pl.ds(n, 1), :] * inv_len
        sub = lax.broadcasted_iota(jnp.int32, (8, channels), 0).astype(f32)
        gam_eight[n] = jnp.exp(-8.0 * rate)
        up_tab[n] = jnp.exp(-rate * sub)
        down_tab[n] = jnp.exp(-rate * (8.0 - sub))
        return 0

    lax.fori_loop(0, 16, table_body, 0)

    pltpu.make_async_copy(pair_l, pair_l, pl_recv).wait()

    def chip_sums(j):
        span = span_t[core, j]
        p_first, _ = ordered(send_a[core, j, 0:8, :], pair_a[core, j, 0:8, :])
        _, c_second = ordered(send_a[core, j, 8:16, :], pair_a[core, j, 8:16, :])
        own_slope, own_lag = send_l[core, j, 0].astype(f32), send_l[core, j, 1].astype(f32)
        pair_slope, pair_lag = pair_l[j, 0].astype(f32), pair_l[j, 1].astype(f32)
        sp_first, sp_second = ordered(own_slope[0:8], pair_slope[0:8])
        sc_first, sc_second = ordered(own_slope[8:16], pair_slope[8:16])
        lags = own_lag + pair_lag
        slopes = [
            span * (sp_first + float(rows) * p_first) + sp_second,
            sc_first + span * (sc_second + float(rows) * c_second),
        ]
        sums = [
            lags[0:8] + c_second * p_first,
            lags[8:16] + (sc_second * p_first + c_second * sp_first),
        ]
        return [jnp.concatenate(tiles, axis=0).astype(bf16) for tiles in (slopes, sums)]

    def store_sums(j, result):
        chip_l[j, 0], chip_l[j, 1] = result

    def send_sums(j):
        to_chip(chip_l, recv_l, j, l_send, l_recv).start()

    by_groups(chip_sums, store_sums, send_sums)
    recv_l[my_chip] = chip_l[my_chip]

    def conv_body(j, _):
        lanes = lanes_of(j, mid)
        taps = jnp.concatenate(
            [
                synth((res_ref[0:8, own], res_ref[8:16, own]), up_tab, own, True)
                for own in [lanes_of(j * (mid // 128) + part, 128) for part in range(mid // 128)]
            ],
            axis=1,
        )
        high = taps.astype(bf16)
        low = (taps - high.astype(f32)).astype(bf16)
        table = fwd_ref[...]
        filt = dot(table, jnp.concatenate([high, high], axis=0)) + dot(table[:, :rows], low)
        prod = prod_h[:, lanes]
        carr = carr_h[:, lanes]
        spec_p = dot(table, jnp.concatenate([prod, prod], axis=0))
        spec_c = dot(table, jnp.concatenate([carr, carr], axis=0))
        fr, fi = filt[:rows], filt[rows:]
        pr, pi = spec_p[:rows], spec_p[rows:]
        cr, ci = spec_c[:rows], spec_c[rows:]
        inverse = inv_ref[...]

        def back_to_rows(real, imag):
            spec = jnp.concatenate([real.astype(bf16), imag.astype(bf16)], axis=0)
            both = dot(inverse, spec)
            return both[:rows] + both[rows:]

        conv_s[:, lanes] = back_to_rows(pr * fr - pi * fi, pr * fi + pi * fr)
        back_s[:, lanes] = back_to_rows(cr * fr + ci * fi, ci * fr - cr * fi)
        return 0

    conv_steps = channels // mid
    conv_early = conv_steps // 4
    lax.fori_loop(0, conv_early, conv_body, 0)

    def wait_bytes(ref, sem, count):
        block = ref.at[pl.ds(0, count)]
        pltpu.make_async_copy(block, block, sem).wait()

    wait_bytes(recv_a, a_recv, chips - 1)
    own_lanes = lanes_of(my_chip, 128)

    def own_pack(block):
        first, second = pack(block)
        return jnp.where(first_core, first, second)

    own_decay = own_pack(rates_ref[:, own_lanes]) * inv_len
    own_res = own_pack(res_ref[:, own_lanes])
    span = jnp.exp(-own_decay * float(2 * rows))
    zero = jnp.zeros((8, 128), f32)

    def up_scan(i, carry):
        state, slope, total, moment = carry
        p_in = recv_a[i, 0:8, :]
        c_in = recv_a[i, 8:16, :]
        send_b[i, 0:8, :] = state
        total = total + c_in * state
        moment = moment + c_in * slope
        slope = span * (slope + state)
        state = span * state + p_in
        return state, slope, total, moment

    _, _, total, moment = lax.fori_loop(0, chips, up_scan, (zero, zero, zero, zero), unroll=4)

    def down_scan(i, state):
        at = chips - 1 - i
        send_b[at, 8:16, :] = state
        return span * state + recv_a[at, 8:16, :]

    lax.fori_loop(0, chips, down_scan, zero, unroll=4)

    def send_b_body(i, _):
        j = chip_at(chips - 1 - i)

        @pl.when(j != my_chip)
        def _():
            pltpu.make_async_remote_copy(
                src_ref=send_b.at[j],
                dst_ref=recv_b.at[core, my_chip],
                send_sem=b_send,
                recv_sem=b_recv.at[my_chip],
                device_id={"seq": 2 * j + core},
                device_id_type=MESH,
            ).start()

        return 0

    lax.fori_loop(0, chips, send_b_body, 0)
    recv_b[core, my_chip] = send_b[my_chip]

    def skip_body(i, acc):
        return acc + recv_a[i, 16:17, :]

    skip_sum = lax.fori_loop(0, chips, skip_body, jnp.zeros((1, 128), f32))

    lax.fori_loop(conv_early, conv_steps, conv_body, 0)

    wait_bytes(recv_l, l_recv, chips - 1)

    def combine_body(i, carry):
        grad_0, grad_1 = carry
        slopes = recv_l[i, 0].astype(f32)
        lags = recv_l[i, 1].astype(f32)
        grad_0 = grad_0 + lags[0:8]
        grad_1 = grad_1 + lags[8:16]
        grad_1 = grad_1 + slopes[8:16] * send_b[i, 0:8, :] + slopes[0:8] * send_b[i, 8:16, :]
        return grad_0, grad_1

    grad_0, grad_1 = lax.fori_loop(
        0, chips, combine_body, (total, float(2 * rows) * moment), unroll=4
    )
    send_g[0:8, :] = grad_0 * inv_len
    send_g[8:16, :] = -own_res * own_decay * grad_1 * inv_len
    send_g[16:17, :] = skip_sum * inv_len

    def send_g_body(step, _):
        pltpu.make_async_remote_copy(
            src_ref=send_g,
            dst_ref=recv_g.at[me_b],
            send_sem=g_send,
            recv_sem=g_recv,
            device_id={"dp": dp_peer(step)},
            device_id_type=MESH,
        ).start()
        return 0

    lax.fori_loop(1, batch, send_g_body, 0)
    recv_g[me_b] = send_g[...]

    def out_copies(j):
        lanes = lanes_of(j, 128)
        return [
            pltpu.make_async_copy(src.at[:, lanes], dst.at[:, lanes], out_sem.at[which])
            for which, (src, dst) in enumerate(((y_out, y_hbm), (dz_out, dz_hbm)))
        ]

    def forward(i):
        j = chip_at(i)
        block = recv_b.at[core, j]

        @pl.when(j != my_chip)
        def _():
            pltpu.make_async_copy(block, block, b_recv.at[j]).wait()

        pair_copy(block, block, f_send, f_recv.at[j]).start()

    ahead = min(3, chips)
    for i in range(ahead):
        forward(i)

    def final_body(i, _):
        @pl.when(i + ahead < chips)
        def _():
            forward(i + ahead)

        j = chip_at(i)
        other = recv_b.at[1 - core, j]
        pltpu.make_async_copy(other, other, f_recv.at[j]).wait()
        lanes = lanes_of(j, 128)
        res = res_ref[:, lanes]
        far = []
        for half, far_core, table, ascending in ((0, 1, up_tab, True), (8, 0, down_tab, False)):
            states = []
            for part in range(2):
                state = recv_b[part, j, half : half + 8, :]
                farther = span_t[part, j] * state + pair_a[part, j, half : half + 8, :]
                states.append(jnp.where(core == far_core, farther, state))
            first, second = states
            low = res[0:8] * jnp.where(left, first, pltpu.roll(second, 64, 1))
            high = res[8:16] * jnp.where(left, pltpu.roll(first, 64, 1), second)
            far.append(synth((low, high), table, lanes, ascending))
        conv = conv_s[:, lanes] + far[0]
        back = back_s[:, lanes] + far[1]
        gain = gain_ref[:, lanes]
        y_out[:, lanes] = (conv.astype(bf16).astype(f32) + gain * prod_f[:, lanes]).astype(bf16)
        dz_out[:, lanes] = (back.astype(bf16).astype(f32) + gain * carr_f[:, lanes]).astype(bf16)
        for copy in out_copies(j):
            copy.start()
        return 0

    lax.fori_loop(0, chips, final_body, 0, unroll=2)

    wait_bytes(recv_g, g_recv, batch - 1)

    def total_body(i, acc):
        return acc + recv_g[i]

    grad_ref[0:17, :] = lax.fori_loop(0, batch, total_body, jnp.zeros((17, 128), f32))

    pltpu.make_async_copy(send_a, send_a, pa_send).wait()
    pltpu.make_async_copy(pair_l, pair_l, pl_send).wait()
    wait_bytes(chip_a, a_send, chips - 1)
    wait_bytes(send_b, b_send, chips - 1)
    wait_bytes(chip_l, l_send, chips - 1)
    wait_bytes(send_b, f_send, chips)
    wait_bytes(recv_g, g_send, batch - 1)

    def drain(j, _):
        for copy in out_copies(j):
            copy.wait()
        return 0

    lax.fori_loop(0, chips, drain, 0)


def gate_kernel(cot, key, value, y, dz, grads, grad_q, grad_k, grad_v, grad_r, grad_l, grad_s):
    dz_now = dz[...].astype(f32)
    grad_q[...] = (cot[...].astype(f32) * y[...].astype(f32)).astype(bf16)
    grad_k[...] = (dz_now * value[...].astype(f32)).astype(bf16)
    grad_v[...] = (dz_now * key[...].astype(f32)).astype(bf16)

    @pl.when(pl.program_id(0) == 0)
    def _():
        for start, out in ((0, grad_r), (8, grad_l)):
            tile = grads[start : start + 8, :]
            out[0:8, :] = tile[:, 0:64]
            out[8:16, :] = pltpu.roll(tile, 64, 1)[:, 0:64]
        grad_s[...] = grads[16:17, 0:64]


def shards(queries, key_branch, value_branch, cotangent, residues, rates, skip_gain):
    groups = lax.axis_size("seq")
    batch = lax.axis_size("dp")
    rows, channels = queries.shape[1:]
    sub_rows = 32
    tables = [jnp.asarray(table) for table in stacked_tables(rows, sub_rows)]
    q, k, v, o = (x[0] for x in (queries, key_branch, value_branch, cotangent))
    hbm = pl.BlockSpec(memory_space=pltpu.HBM)
    big = pltpu.VMEM((rows, channels), f32)
    half = pltpu.VMEM((rows, channels), bf16)
    dma = pltpu.SemaphoreType.DMA
    chips = groups // 2
    chunks = chips // min(4, chips)
    y, dz, grads = pl.pallas_call(
        functools.partial(main_kernel, rows, channels, groups, batch),
        out_shape=[
            jax.ShapeDtypeStruct((rows, channels), bf16),
            jax.ShapeDtypeStruct((rows, channels), bf16),
            jax.ShapeDtypeStruct((24, 128), f32),
        ],
        in_specs=[hbm] * 11,
        out_specs=[hbm, hbm, pl.BlockSpec(memory_space=pltpu.VMEM)],
        scratch_shapes=[pltpu.VMEM((16, channels), f32)] * 2
        + [pltpu.VMEM((1, channels), f32)]
        + [pltpu.VMEM(table.shape, bf16) for table in tables]
        + [half] * 6
        + [big] * 4
        + [pltpu.VMEM((sub_rows, channels), f32)]
        + [pltpu.VMEM((16, 8, channels), f32)] * 2
        + [pltpu.VMEM((16, channels), f32)] * 2
        + [pltpu.VMEM((rows // sub_rows, 16, channels), f32)] * 4
        + [pltpu.VMEM((16, channels), f32)] * 2
        + [pltpu.VMEM((16, 1, channels), f32)]
        + [half] * 2
        + [pltpu.VMEM((2, chips, 8, 128), f32)]
        + [pltpu.VMEM((2, chips, 17, 128), f32)] * 2
        + [pltpu.VMEM((chips, 17, 128), f32)] * 2
        + [pltpu.VMEM((chips, 16, 128), f32)]
        + [pltpu.VMEM((2, chips, 16, 128), f32)]
        + [pltpu.VMEM((2, chips, 2, 16, 128), bf16)]
        + [pltpu.VMEM((chips, 2, 16, 128), bf16)] * 3
        + [pltpu.VMEM((17, 128), f32), pltpu.VMEM((batch, 17, 128), f32)]
        + [dma((4, chunks)), dma((7,)), dma((2,))]
        + [dma] * 5
        + [dma((chips,)), dma, dma((chips,))]
        + [dma] * 6,
        compiler_params=pltpu.CompilerParams(
            collective_id=0, has_side_effects=True, vmem_limit_bytes=62 * 2**20
        ),
        name="hyena_main",
    )(q, k, v, o, residues, rates, skip_gain[None, :], *tables)
    tile = min(64, rows)
    rowed = pl.BlockSpec((tile, channels), lambda i: (i, 0))

    def whole(*shape):
        return pl.BlockSpec(shape, lambda i: (0, 0))

    wide16 = jax.ShapeDtypeStruct((rows, channels), bf16)
    gq, gk, gv, gr, gl, gs = pl.pallas_call(
        gate_kernel,
        grid=(rows // tile,),
        out_shape=[wide16] * 3
        + [jax.ShapeDtypeStruct((16, 64), f32)] * 2
        + [jax.ShapeDtypeStruct((1, 64), f32)],
        in_specs=[rowed] * 5 + [whole(24, 128)],
        out_specs=[rowed] * 3 + [whole(16, 64), whole(16, 64), whole(1, 64)],
        compiler_params=pltpu.CompilerParams(vmem_limit_bytes=62 * 2**20),
        name="hyena_gate",
    )(o, k, v, y, dz, grads)
    return gq[None], gk[None], gv[None], gr, gl, gs[0]


def solution(mesh):
    row_spec = P("dp", "seq", None)
    return jax.shard_map(
        shards,
        mesh=mesh,
        in_specs=(row_spec,) * 4 + (P(),) * 3,
        out_specs=(row_spec,) * 3 + (P(None, "seq"), P(None, "seq"), P("seq")),
        check_vma=False,
    )
```

```python
import functools

import jax
import jax.numpy as jnp
import ml_dtypes
import numpy as np
from jax import lax
from jax.experimental import pallas as pl
from jax.experimental.pallas import tpu as pltpu
from jax.sharding import PartitionSpec as P

MESH = pl.DeviceIdType.MESH
f32 = jnp.float32
bf16 = jnp.bfloat16


def split_table(table):
    high = table.astype(ml_dtypes.bfloat16)
    low = (table - high.astype(np.float64)).astype(ml_dtypes.bfloat16)
    return high, low


def dft_tables(rows):
    odd = 2 * np.arange(rows)[:, None] + 1
    angle = np.pi / (2 * rows) * (odd * np.arange(rows)[None, :] % (4 * rows))
    forward = np.concatenate([np.cos(angle), -np.sin(angle)], axis=0)
    inverse = np.concatenate([np.cos(angle).T, -np.sin(angle).T], axis=1) / rows
    return forward, inverse


def stacked_tables(rows, sub_rows):
    forward, inverse = dft_tables(rows)
    sub_fwd, sub_inv = dft_tables(sub_rows)
    parts = rows // sub_rows
    blocks = np.zeros((2, sub_rows, parts, parts, sub_rows))
    for part in range(parts):
        blocks[:, :, part, part, :] = sub_fwd.reshape(2, sub_rows, sub_rows)
    blocks = blocks.transpose(0, 2, 1, 3, 4).reshape(2 * rows, rows)
    fwd = np.concatenate(split_table(forward), axis=1)
    inv = np.concatenate(split_table(inverse), axis=0)
    fwd_sub = np.concatenate(split_table(blocks), axis=1)
    inv_sub = np.concatenate(split_table(sub_inv), axis=0)
    return fwd, inv, fwd_sub, inv_sub


def main_kernel(
    rows,
    channels,
    groups,
    batch,
    q_hbm,
    k_hbm,
    v_hbm,
    o_hbm,
    res_hbm,
    rates_hbm,
    gain_hbm,
    fwd_hbm,
    inv_hbm,
    fsub_hbm,
    isub_hbm,
    y_hbm,
    dz_hbm,
    grad_ref,
    res_ref,
    rates_ref,
    gain_ref,
    fwd_ref,
    inv_ref,
    fsub_ref,
    isub_ref,
    q_in,
    k_in,
    v_in,
    o_in,
    prod_h,
    carr_h,
    prod_f,
    carr_f,
    conv_s,
    back_s,
    lag_s,
    up_tab,
    down_tab,
    gam_one,
    gam_sub,
    sub_s,
    sub_b,
    sub_s1,
    sub_b1,
    lag_0,
    lag_1,
    gam_eight,
    y_out,
    dz_out,
    span_t,
    send_a,
    pair_a,
    chip_a,
    recv_a,
    send_b,
    recv_b,
    send_l,
    pair_l,
    chip_l,
    recv_l,
    send_g,
    recv_g,
    in_sem,
    small_sem,
    out_sem,
    pa_send,
    pa_recv,
    a_send,
    a_recv,
    b_send,
    b_recv,
    f_send,
    f_recv,
    pl_send,
    pl_recv,
    l_send,
    l_recv,
    g_send,
    g_recv,
):
    length = rows * groups
    inv_len = 1.0 / length
    sub_rows = isub_ref.shape[0] // 2
    parts = rows // sub_rows
    ny = min(4, groups // 2)
    nx = groups // (2 * ny)
    chunks = nx
    wide = channels // chunks
    mid = min(512, channels)
    me = lax.axis_index("seq")
    me_b = lax.axis_index("dp")

    chips = groups // 2
    my_chip = me // 2
    core = lax.rem(me, 2)
    first_core = core == 0
    sibling = me + 1 - 2 * core

    def dp_peer(step):
        return lax.rem(me_b + step, batch)

    def lanes_of(index, size):
        return pl.ds(pl.multiple_of(index * size, size), size)

    my_x = me // (2 * ny)
    my_y = lax.rem(me // 2, ny)

    def spread(index, size):
        return lax.rem(index * (index + 1) // 2, size)

    def chip_at(index):
        x = lax.rem(my_x + spread(lax.rem(index, nx), nx), nx)
        y = lax.rem(my_y + spread(index // nx, ny), ny)
        return x * ny + y

    def chunk_at(step):
        return lax.rem(my_x + (chunks - 1 - step) * (chunks - step) // 2, chunks)

    def in_copies(step):
        lanes = lanes_of(chunk_at(step), wide)
        return [
            pltpu.make_async_copy(src.at[:, lanes], dst.at[:, lanes], in_sem.at[which, step])
            for which, (src, dst) in enumerate(
                ((k_hbm, k_in), (v_hbm, v_in), (o_hbm, o_in), (q_hbm, q_in))
            )
        ]

    small = [
        pltpu.make_async_copy(src, dst, small_sem.at[which])
        for which, (src, dst) in enumerate(
            (
                (rates_hbm, rates_ref),
                (res_hbm, res_ref),
                (gain_hbm, gain_ref),
                (fwd_hbm, fwd_ref),
                (inv_hbm, inv_ref),
                (fsub_hbm, fsub_ref),
                (isub_hbm, isub_ref),
            )
        )
    ]
    for copy in small[:2]:
        copy.start()
    ready = min(2, chunks)
    for step in range(ready):
        for copy in in_copies(step):
            copy.start()

    barrier = pltpu.get_barrier_semaphore()

    def greet_chip(step, _):
        peer = 2 * lax.rem(my_chip + step, chips) + core
        pl.semaphore_signal(barrier, inc=1, device_id={"seq": peer}, device_id_type=MESH)
        return 0

    def greet_dp(step, _):
        pl.semaphore_signal(barrier, inc=1, device_id={"dp": dp_peer(step)}, device_id_type=MESH)
        return 0

    lax.fori_loop(1, chips, greet_chip, 0)
    pl.semaphore_signal(barrier, inc=1, device_id={"seq": sibling}, device_id_type=MESH)
    lax.fori_loop(1, batch, greet_dp, 0)

    for copy in small[:2]:
        copy.wait()
    decay_all = rates_ref[...] * inv_len
    gam_one[...] = jnp.exp(-decay_all)
    gam_sub[...] = jnp.exp(-float(sub_rows) * decay_all)
    lane = lax.broadcasted_iota(jnp.int32, (8, 128), 1)
    left = lane < 64

    def pack(block):
        top = block[0:8]
        low = block[8:16]
        return (
            jnp.where(left, top, pltpu.roll(low, 64, 1)),
            jnp.where(left, pltpu.roll(top, 64, 1), low),
        )

    def horner(jobs, lanes, width):
        gamma = gam_one[:, lanes]
        totals = [jnp.zeros((16, width), f32)] * len(jobs)
        row = lax.broadcasted_iota(jnp.int32, (8, width), 0).astype(f32)
        for i in range(sub_rows // 8):
            at = sub_rows - 8 - i * 8
            blocks = []
            for ref, base, up, weighted in jobs:
                start = pl.multiple_of(base + (i * 8 if up else at), 8)
                block = ref[pl.ds(start, 8), lanes]
                if weighted:
                    block = block * (float(sub_rows - i * 8) - row if up else float(at) + row)
                blocks.append(block)
            for r in range(8):
                for which, (job, block) in enumerate(zip(jobs, blocks)):
                    x = block[r : r + 1] if job[2] else block[7 - r : 8 - r]
                    totals[which] = totals[which] * gamma + x
        return [t * gamma if job[2] else t for t, job in zip(totals, jobs)]

    for step in range(chunks):
        chunk = chunk_at(step)
        lanes = lanes_of(chunk, wide)
        for copy in in_copies(step):
            copy.wait()
        later = in_copies(step + ready) if step + ready < chunks else []
        for copy in later + (small[2:] if step == chunks - 1 else []):
            copy.start()
        prod = (k_in[:, lanes].astype(f32) * v_in[:, lanes].astype(f32)).astype(bf16)
        carr = (o_in[:, lanes].astype(f32) * q_in[:, lanes].astype(f32)).astype(bf16)
        prod_h[:, lanes] = prod
        carr_h[:, lanes] = carr
        prod_32 = prod.astype(f32)
        carr_32 = carr.astype(f32)
        prod_f[:, lanes] = prod_32
        carr_f[:, lanes] = carr_32
        skip = jnp.sum(prod_32 * carr_32, axis=0, keepdims=True)

        def state_body(part, _):
            base = pl.multiple_of(part * sub_rows, sub_rows)
            sub_s[part, :, lanes], sub_b[part, :, lanes] = horner(
                [(prod_f, base, True, False), (carr_f, base, False, False)], lanes, wide
            )
            return 0

        lax.fori_loop(0, parts, state_body, 0)
        ratio = gam_sub[:, lanes]
        state_p = sub_s[0, :, lanes]
        state_c = sub_b[parts - 1, :, lanes]
        for part in range(1, parts):
            state_p = state_p * ratio + sub_s[part, :, lanes]
            state_c = state_c * ratio + sub_b[parts - 1 - part, :, lanes]
        for part in range(wide // 128):
            cut = slice(part * 128, part * 128 + 128)
            pair = chunk * (wide // 128) + part
            for half, (p_tile, c_tile) in enumerate(zip(pack(state_p[:, cut]), pack(state_c[:, cut]))):
                send_a[half, pair, 0:8, :] = p_tile
                send_a[half, pair, 8:16, :] = c_tile
            row = skip[:, cut]
            send_a[0, pair, 16:17, :] = row
            send_a[1, pair, 16:17, :] = pltpu.roll(row, 64, 1)

    pl.semaphore_wait(barrier, chips + batch - 1)

    def pair_copy(src, dst, send_sem, recv_sem):
        return pltpu.make_async_remote_copy(
            src_ref=src,
            dst_ref=dst,
            send_sem=send_sem,
            recv_sem=recv_sem,
            device_id={"seq": sibling},
            device_id_type=MESH,
        )

    pair_copy(send_a, pair_a, pa_send, pa_recv).start()

    def span_body(j, _):
        lanes = lanes_of(j, 128)
        span = jnp.exp(rates_ref[:, lanes] * (-inv_len * float(rows)))
        span_t[0, j], span_t[1, j] = pack(span)
        return 0

    lax.fori_loop(0, chips, span_body, 0, unroll=4)
    pltpu.make_async_copy(pair_a, pair_a, pa_recv).wait()

    def ordered(own, other):
        return jnp.where(first_core, own, other), jnp.where(first_core, other, own)

    def to_chip(src, dst, peer_chip, send_sem, recv_sem):
        return pltpu.make_async_remote_copy(
            src_ref=src.at[peer_chip],
            dst_ref=dst.at[my_chip],
            send_sem=send_sem,
            recv_sem=recv_sem,
            device_id={"seq": 2 * peer_chip + core},
            device_id_type=MESH,
        )

    group = min(4, chips)

    def by_groups(compute, store, send):
        def body(i, _):
            at = [chip_at(chips - 1 - (group * i + part)) for part in range(group)]
            results = [compute(j) for j in at]
            for j, result in zip(at, results):
                store(j, result)
            for j in at:
                pl.when(j != my_chip)(functools.partial(send, j))
            return 0

        lax.fori_loop(0, chips // group, body, 0)

    def chip_states(j):
        span = span_t[core, j]
        own, other = send_a[core, j], pair_a[core, j]
        p_first, p_second = ordered(own[0:8], other[0:8])
        c_first, c_second = ordered(own[8:16], other[8:16])
        return span * p_first + p_second, c_first + span * c_second, own[16:17] + other[16:17]

    def store_states(j, result):
        chip_a[j, 0:8, :], chip_a[j, 8:16, :], chip_a[j, 16:17, :] = result

    def send_states(j):
        to_chip(chip_a, recv_a, j, a_send, a_recv).start()

    by_groups(chip_states, store_states, send_states)
    recv_a[my_chip] = chip_a[my_chip]


    def synth(coefs, table, lanes, ascending):
        count = rows // 8
        waves = [table[n, :, lanes] * coefs[n // 8][n % 8 : n % 8 + 1] for n in range(16)]
        ratios = [jnp.broadcast_to(gam_eight[n, :, lanes], (8, 128)) for n in range(16)]
        blocks = []
        for order in range(count):
            terms = waves
            while len(terms) > 1:
                terms = [terms[i] + terms[i + 1] for i in range(0, len(terms), 2)]
            blocks.append(terms[0])
            if order < count - 1:
                waves = [wave * ratio for wave, ratio in zip(waves, ratios)]
        return jnp.concatenate(blocks if ascending else blocks[::-1], axis=0)

    def dot(a, b):
        return jnp.dot(a, b, preferred_element_type=f32)

    for copy in small[2:]:
        copy.wait()

    def lag_sums(j):
        lanes = lanes_of(j, mid)
        jobs = [(lag_s, 0, False, False), (lag_s, 0, False, True)]
        lag_0[:, lanes], lag_1[:, lanes] = horner(jobs, lanes, mid)

    def lag_body(j, _):
        lanes = lanes_of(j, mid)
        table = fsub_ref[...]
        prod = prod_h[:, lanes]
        carr = carr_h[:, lanes]
        spec_p = dot(table, jnp.concatenate([prod, prod], axis=0))
        spec_c = dot(table, jnp.concatenate([carr, carr], axis=0))
        real = jnp.zeros((sub_rows, mid), f32)
        imag = jnp.zeros((sub_rows, mid), f32)
        for part in range(parts):
            lo = part * sub_rows
            pr, pi = spec_p[lo : lo + sub_rows], spec_p[rows + lo : rows + lo + sub_rows]
            cr, ci = spec_c[lo : lo + sub_rows], spec_c[rows + lo : rows + lo + sub_rows]
            real = real + (cr * pr + ci * pi)
            imag = imag + (ci * pr - cr * pi)
        both = dot(isub_ref[...], jnp.concatenate([real.astype(bf16), imag.astype(bf16)], axis=0))
        lag_s[:, lanes] = both[:sub_rows] + both[sub_rows:]
        for part in range(0, parts, 2):
            jobs = []
            for now in (part, part + 1):
                jobs.append((prod_f, now * sub_rows, True, True))
                jobs.append((carr_f, now * sub_rows, False, True))
            slopes = horner(jobs, lanes, mid)
            for now in range(2):
                sub_s1[part + now, :, lanes] = slopes[2 * now]
                sub_b1[part + now, :, lanes] = slopes[2 * now + 1]
        lag_sums(jnp.maximum(j - 1, 0))
        return 0

    lag_s[:, 0:mid] = jnp.zeros((sub_rows, mid), f32)
    lax.fori_loop(0, channels // mid, lag_body, 0)
    lag_sums(channels // mid - 1)

    def moments_of(pair):
        own = lanes_of(pair, 128)
        ratio = gam_sub[:, own]
        total_0, total_1 = lag_0[:, own], lag_1[:, own]
        p_state = [sub_s[q, :, own] for q in range(parts)]
        p_slope = [sub_s1[q, :, own] for q in range(parts)]
        c_states = [sub_b[q, :, own] for q in range(parts)]
        c_slopes = [sub_b1[q, :, own] for q in range(parts)]
        state, slope = p_state[0], p_slope[0]
        for q in range(1, parts):
            total_0 = total_0 + c_states[q] * state
            total_1 = total_1 + (c_slopes[q] * state + c_states[q] * slope)
            slope = ratio * (slope + float(sub_rows) * state) + p_slope[q]
            state = ratio * state + p_state[q]
        c_slope, c_state = c_slopes[-1], c_states[-1]
        for q in range(parts - 2, -1, -1):
            c_slope = ratio * (c_slope + float(sub_rows) * c_state) + c_slopes[q]
            c_state = ratio * c_state + c_states[q]
        tiles = [pack(x) for x in (slope, c_slope, total_0, total_1)]
        return [
            jnp.concatenate([tiles[2 * which][half], tiles[2 * which + 1][half]], axis=0).astype(bf16)
            for half in range(2)
            for which in range(2)
        ]

    def moments_body(i, _):
        pairs = [group * i + part for part in range(group)]
        results = [moments_of(pair) for pair in pairs]
        for pair, result in zip(pairs, results):
            for half in range(2):
                for which in range(2):
                    send_l[half, pair, which] = result[2 * half + which]
        return 0

    lax.fori_loop(0, chips // group, moments_body, 0)

    pair_copy(send_l.at[1 - core], pair_l, pl_send, pl_recv).start()

    def table_body(n, _):
        rate = rates_ref[pl.ds(n, 1), :] * inv_len
        sub = lax.broadcasted_iota(jnp.int32, (8, channels), 0).astype(f32)
        gam_eight[n] = jnp.exp(-8.0 * rate)
        up_tab[n] = jnp.exp(-rate * sub)
        down_tab[n] = jnp.exp(-rate * (8.0 - sub))
        return 0

    lax.fori_loop(0, 16, table_body, 0)

    pltpu.make_async_copy(pair_l, pair_l, pl_recv).wait()

    def chip_sums(j):
        span = span_t[core, j]
        p_first, _ = ordered(send_a[core, j, 0:8, :], pair_a[core, j, 0:8, :])
        _, c_second = ordered(send_a[core, j, 8:16, :], pair_a[core, j, 8:16, :])
        own_slope, own_lag = send_l[core, j, 0].astype(f32), send_l[core, j, 1].astype(f32)
        pair_slope, pair_lag = pair_l[j, 0].astype(f32), pair_l[j, 1].astype(f32)
        sp_first, sp_second = ordered(own_slope[0:8], pair_slope[0:8])
        sc_first, sc_second = ordered(own_slope[8:16], pair_slope[8:16])
        lags = own_lag + pair_lag
        slopes = [
            span * (sp_first + float(rows) * p_first) + sp_second,
            sc_first + span * (sc_second + float(rows) * c_second),
        ]
        sums = [
            lags[0:8] + c_second * p_first,
            lags[8:16] + (sc_second * p_first + c_second * sp_first),
        ]
        return [jnp.concatenate(tiles, axis=0).astype(bf16) for tiles in (slopes, sums)]

    def store_sums(j, result):
        chip_l[j, 0], chip_l[j, 1] = result

    def send_sums(j):
        to_chip(chip_l, recv_l, j, l_send, l_recv).start()

    by_groups(chip_sums, store_sums, send_sums)
    recv_l[my_chip] = chip_l[my_chip]

    def conv_body(j, _):
        lanes = lanes_of(j, mid)
        taps = jnp.concatenate(
            [
                synth((res_ref[0:8, own], res_ref[8:16, own]), up_tab, own, True)
                for own in [lanes_of(j * (mid // 128) + part, 128) for part in range(mid // 128)]
            ],
            axis=1,
        )
        high = taps.astype(bf16)
        low = (taps - high.astype(f32)).astype(bf16)
        table = fwd_ref[...]
        filt = dot(table, jnp.concatenate([high, high], axis=0)) + dot(table[:, :rows], low)
        prod = prod_h[:, lanes]
        carr = carr_h[:, lanes]
        spec_p = dot(table, jnp.concatenate([prod, prod], axis=0))
        spec_c = dot(table, jnp.concatenate([carr, carr], axis=0))
        fr, fi = filt[:rows], filt[rows:]
        pr, pi = spec_p[:rows], spec_p[rows:]
        cr, ci = spec_c[:rows], spec_c[rows:]
        inverse = inv_ref[...]

        def back_to_rows(real, imag):
            spec = jnp.concatenate([real.astype(bf16), imag.astype(bf16)], axis=0)
            both = dot(inverse, spec)
            return both[:rows] + both[rows:]

        conv_s[:, lanes] = back_to_rows(pr * fr - pi * fi, pr * fi + pi * fr)
        back_s[:, lanes] = back_to_rows(cr * fr + ci * fi, ci * fr - cr * fi)
        return 0

    conv_steps = channels // mid
    conv_early = conv_steps // 4
    lax.fori_loop(0, conv_early, conv_body, 0)

    def wait_bytes(ref, sem, count):
        block = ref.at[pl.ds(0, count)]
        pltpu.make_async_copy(block, block, sem).wait()

    wait_bytes(recv_a, a_recv, chips - 1)
    own_lanes = lanes_of(my_chip, 128)

    def own_pack(block):
        first, second = pack(block)
        return jnp.where(first_core, first, second)

    own_decay = own_pack(rates_ref[:, own_lanes]) * inv_len
    own_res = own_pack(res_ref[:, own_lanes])
    span = jnp.exp(-own_decay * float(2 * rows))
    zero = jnp.zeros((8, 128), f32)

    def up_scan(i, carry):
        state, slope, total, moment = carry
        p_in = recv_a[i, 0:8, :]
        c_in = recv_a[i, 8:16, :]
        send_b[i, 0:8, :] = state
        total = total + c_in * state
        moment = moment + c_in * slope
        slope = span * (slope + state)
        state = span * state + p_in
        return state, slope, total, moment

    _, _, total, moment = lax.fori_loop(0, chips, up_scan, (zero, zero, zero, zero), unroll=4)

    def down_scan(i, state):
        at = chips - 1 - i
        send_b[at, 8:16, :] = state
        return span * state + recv_a[at, 8:16, :]

    lax.fori_loop(0, chips, down_scan, zero, unroll=4)

    def send_b_body(i, _):
        j = chip_at(chips - 1 - i)

        @pl.when(j != my_chip)
        def _():
            pltpu.make_async_remote_copy(
                src_ref=send_b.at[j],
                dst_ref=recv_b.at[core, my_chip],
                send_sem=b_send,
                recv_sem=b_recv.at[my_chip],
                device_id={"seq": 2 * j + core},
                device_id_type=MESH,
            ).start()

        return 0

    lax.fori_loop(0, chips, send_b_body, 0)
    recv_b[core, my_chip] = send_b[my_chip]

    def skip_body(i, acc):
        return acc + recv_a[i, 16:17, :]

    skip_sum = lax.fori_loop(0, chips, skip_body, jnp.zeros((1, 128), f32))

    lax.fori_loop(conv_early, conv_steps, conv_body, 0)

    wait_bytes(recv_l, l_recv, chips - 1)

    def combine_body(i, carry):
        grad_0, grad_1 = carry
        slopes = recv_l[i, 0].astype(f32)
        lags = recv_l[i, 1].astype(f32)
        grad_0 = grad_0 + lags[0:8]
        grad_1 = grad_1 + lags[8:16]
        grad_1 = grad_1 + slopes[8:16] * send_b[i, 0:8, :] + slopes[0:8] * send_b[i, 8:16, :]
        return grad_0, grad_1

    grad_0, grad_1 = lax.fori_loop(
        0, chips, combine_body, (total, float(2 * rows) * moment), unroll=8
    )
    send_g[0:8, :] = grad_0 * inv_len
    send_g[8:16, :] = -own_res * own_decay * grad_1 * inv_len
    send_g[16:17, :] = skip_sum * inv_len

    def send_g_body(step, _):
        pltpu.make_async_remote_copy(
            src_ref=send_g,
            dst_ref=recv_g.at[me_b],
            send_sem=g_send,
            recv_sem=g_recv,
            device_id={"dp": dp_peer(step)},
            device_id_type=MESH,
        ).start()
        return 0

    lax.fori_loop(1, batch, send_g_body, 0)
    recv_g[me_b] = send_g[...]

    def out_copies(j):
        lanes = lanes_of(j, 128)
        return [
            pltpu.make_async_copy(src.at[:, lanes], dst.at[:, lanes], out_sem.at[which])
            for which, (src, dst) in enumerate(((y_out, y_hbm), (dz_out, dz_hbm)))
        ]

    def forward(i):
        j = chip_at(i)
        block = recv_b.at[core, j]

        @pl.when(j != my_chip)
        def _():
            pltpu.make_async_copy(block, block, b_recv.at[j]).wait()

        pair_copy(block, block, f_send, f_recv.at[j]).start()

    ahead = min(3, chips)
    for i in range(ahead):
        forward(i)

    def final_body(i, _):
        @pl.when(i + ahead < chips)
        def _():
            forward(i + ahead)

        j = chip_at(i)
        other = recv_b.at[1 - core, j]
        pltpu.make_async_copy(other, other, f_recv.at[j]).wait()
        lanes = lanes_of(j, 128)
        res = res_ref[:, lanes]
        far = []
        for half, far_core, table, ascending in ((0, 1, up_tab, True), (8, 0, down_tab, False)):
            states = []
            for part in range(2):
                state = recv_b[part, j, half : half + 8, :]
                farther = span_t[part, j] * state + pair_a[part, j, half : half + 8, :]
                states.append(jnp.where(core == far_core, farther, state))
            first, second = states
            low = res[0:8] * jnp.where(left, first, pltpu.roll(second, 64, 1))
            high = res[8:16] * jnp.where(left, pltpu.roll(first, 64, 1), second)
            far.append(synth((low, high), table, lanes, ascending))
        conv = conv_s[:, lanes] + far[0]
        back = back_s[:, lanes] + far[1]
        gain = gain_ref[:, lanes]
        y_out[:, lanes] = (conv.astype(bf16).astype(f32) + gain * prod_f[:, lanes]).astype(bf16)
        dz_out[:, lanes] = (back.astype(bf16).astype(f32) + gain * carr_f[:, lanes]).astype(bf16)
        for copy in out_copies(j):
            copy.start()
        return 0

    lax.fori_loop(0, chips, final_body, 0, unroll=2)

    pltpu.make_async_copy(send_a, send_a, pa_send).wait()
    pltpu.make_async_copy(pair_l, pair_l, pl_send).wait()
    wait_bytes(chip_a, a_send, chips - 1)
    wait_bytes(send_b, b_send, chips - 1)
    wait_bytes(chip_l, l_send, chips - 1)
    wait_bytes(send_b, f_send, chips)
    wait_bytes(recv_g, g_send, batch - 1)

    def drain(j, _):
        for copy in out_copies(j):
            copy.wait()
        return 0

    lax.fori_loop(0, chips, drain, 0)

    wait_bytes(recv_g, g_recv, batch - 1)

    def total_body(i, acc):
        return acc + recv_g[i]

    grad_ref[0:17, :] = lax.fori_loop(
        0, batch, total_body, jnp.zeros((17, 128), f32), unroll=True
    )


def gate_kernel(cot, key, value, y, dz, grads, grad_q, grad_k, grad_v, grad_r, grad_l, grad_s):
    dz_now = dz[...].astype(f32)
    grad_q[...] = (cot[...].astype(f32) * y[...].astype(f32)).astype(bf16)
    grad_k[...] = (dz_now * value[...].astype(f32)).astype(bf16)
    grad_v[...] = (dz_now * key[...].astype(f32)).astype(bf16)

    @pl.when(pl.program_id(0) == 0)
    def _():
        for start, out in ((0, grad_r), (8, grad_l)):
            tile = grads[start : start + 8, :]
            out[0:8, :] = tile[:, 0:64]
            out[8:16, :] = pltpu.roll(tile, 64, 1)[:, 0:64]
        grad_s[...] = grads[16:17, 0:64]


def shards(queries, key_branch, value_branch, cotangent, residues, rates, skip_gain):
    groups = lax.axis_size("seq")
    batch = lax.axis_size("dp")
    rows, channels = queries.shape[1:]
    sub_rows = 32
    tables = [jnp.asarray(table) for table in stacked_tables(rows, sub_rows)]
    q, k, v, o = (x[0] for x in (queries, key_branch, value_branch, cotangent))
    hbm = pl.BlockSpec(memory_space=pltpu.HBM)
    big = pltpu.VMEM((rows, channels), f32)
    half = pltpu.VMEM((rows, channels), bf16)
    dma = pltpu.SemaphoreType.DMA
    chips = groups // 2
    chunks = chips // min(4, chips)
    y, dz, grads = pl.pallas_call(
        functools.partial(main_kernel, rows, channels, groups, batch),
        out_shape=[
            jax.ShapeDtypeStruct((rows, channels), bf16),
            jax.ShapeDtypeStruct((rows, channels), bf16),
            jax.ShapeDtypeStruct((24, 128), f32),
        ],
        in_specs=[hbm] * 11,
        out_specs=[hbm, hbm, pl.BlockSpec(memory_space=pltpu.VMEM)],
        scratch_shapes=[pltpu.VMEM((16, channels), f32)] * 2
        + [pltpu.VMEM((1, channels), f32)]
        + [pltpu.VMEM(table.shape, bf16) for table in tables]
        + [half] * 6
        + [big] * 4
        + [pltpu.VMEM((sub_rows, channels), f32)]
        + [pltpu.VMEM((16, 8, channels), f32)] * 2
        + [pltpu.VMEM((16, channels), f32)] * 2
        + [pltpu.VMEM((rows // sub_rows, 16, channels), f32)] * 4
        + [pltpu.VMEM((16, channels), f32)] * 2
        + [pltpu.VMEM((16, 1, channels), f32)]
        + [half] * 2
        + [pltpu.VMEM((2, chips, 8, 128), f32)]
        + [pltpu.VMEM((2, chips, 17, 128), f32)] * 2
        + [pltpu.VMEM((chips, 17, 128), f32)] * 2
        + [pltpu.VMEM((chips, 16, 128), f32)]
        + [pltpu.VMEM((2, chips, 16, 128), f32)]
        + [pltpu.VMEM((2, chips, 2, 16, 128), bf16)]
        + [pltpu.VMEM((chips, 2, 16, 128), bf16)] * 3
        + [pltpu.VMEM((17, 128), f32), pltpu.VMEM((batch, 17, 128), f32)]
        + [dma((4, chunks)), dma((7,)), dma((2,))]
        + [dma] * 5
        + [dma((chips,)), dma, dma((chips,))]
        + [dma] * 6,
        compiler_params=pltpu.CompilerParams(
            collective_id=0, has_side_effects=True, vmem_limit_bytes=62 * 2**20
        ),
        name="hyena_main",
    )(q, k, v, o, residues, rates, skip_gain[None, :], *tables)
    tile = min(64, rows)
    rowed = pl.BlockSpec((tile, channels), lambda i: (i, 0))

    def whole(*shape):
        return pl.BlockSpec(shape, lambda i: (0, 0))

    wide16 = jax.ShapeDtypeStruct((rows, channels), bf16)
    gq, gk, gv, gr, gl, gs = pl.pallas_call(
        gate_kernel,
        grid=(rows // tile,),
        out_shape=[wide16] * 3
        + [jax.ShapeDtypeStruct((16, 64), f32)] * 2
        + [jax.ShapeDtypeStruct((1, 64), f32)],
        in_specs=[rowed] * 5 + [whole(24, 128)],
        out_specs=[rowed] * 3 + [whole(16, 64), whole(16, 64), whole(1, 64)],
        compiler_params=pltpu.CompilerParams(vmem_limit_bytes=62 * 2**20),
        name="hyena_gate",
    )(o, k, v, y, dz, grads)
    return gq[None], gk[None], gv[None], gr, gl, gs[0]


def solution(mesh):
    row_spec = P("dp", "seq", None)
    return jax.shard_map(
        shards,
        mesh=mesh,
        in_specs=(row_spec,) * 4 + (P(),) * 3,
        out_specs=(row_spec,) * 3 + (P(None, "seq"), P(None, "seq"), P("seq")),
        check_vma=False,
    )
```
